32 devices in a mesh: groups: 16 (over z, y, x), mp: 2 (over core).
Axes of the slice: x: 2, y: 2, z: 4, core: 2. Of those that a mesh axis runs over, the one named last changes fastest.
Arguments:
- latents: float32 [1536, 256], P('groups', 'mp'), may hold values from -6 to 6
- tile_slot: int32 [1536], replicated, may hold values from 0 to 1535, as said below
- live: int32 [16], replicated, may hold values from 192 to 384, as said below
- partner: int32 [16], replicated, may hold values from 0 to 15, as said below
- text_states: bfloat16 [16, 2, 154, 2432], P('groups'), may hold values from -6 to 6
- modulation: float32 [16, 2, 5, 2432], P('groups'), may hold values from -3 to 3
- w_embed: bfloat16 [64, 2432], replicated, may hold values from -0.75 to 0.75
- w_qkv: bfloat16 [2432, 3, 1280], P(None, None, 'mp'), may hold values from -0.125 to 0.125
- w_text_kv: bfloat16 [2432, 2, 1280], P(None, None, 'mp'), may hold values from -0.125 to 0.125
- w_out: bfloat16 [1280, 2432], P('mp'), may hold values from -0.15625 to 0.15625
- w_final: bfloat16 [2432, 64], replicated, may hold values from -0.125 to 0.125
- norm_gains: float32 [3, 64], replicated, may hold values from 0.5 to 24
Outputs:
- new_latents: float32 [1536, 256], P('groups', 'mp')
The draws below stay inside these ranges and needn't reach their ends.
Inputs may be any that keep to these rules, and one draw needn't show every extreme that they name: `tile_slot`: every slot appears once; the tiles of one group go to any one group at most 6 times, and exactly 6 times for some pairs of groups. `live`: two groups that share a request hold equal counts; some group is full in every draw. partner[g] is g or g with its lowest bit flipped, and partner[partner[g]] = g; some pair shares a request in every draw.
All inputs are finite; a program needn't handle non-finite values.
Results may differ from the reference program's by a relative error of at most 0.012.
The reference program's roundings to bfloat16 on the way (of `normed`, `query`, `weights`, `attended` and `final`) count: a program that leaves them out, or rounds other values in their place, can miss the bound.
Values may be sent and summed in bfloat16 or wider, within the bound.
No kernel may reach another device: no remote copies, remote signals or barrier semaphores. Data moves between devices by JAX's collectives and lax.ppermute only.
A program may use at most 128 MiB of HBM per device.

```python
import math
import jax
import jax.numpy as jnp
from jax import lax

D = 2432
HEADS = 20
HEAD = 64
CH = 64
TEXT = 154
ROWS = 384
TILE = 4
GROUPS = 16
TILES = 96
CAP = 6
N_GROUPS = 16
N_MP = 2


def draw_tile_slot(key, part):
    first_key, second_key = jax.random.split(jax.random.fold_in(key, 11))
    mixed_shifts = jax.random.permutation(first_key, GROUPS).astype(jnp.int32)
    places = jnp.arange(GROUPS, dtype=jnp.int32)
    priority = jnp.where(mixed_shifts == 1, -3, jnp.where(mixed_shifts == GROUPS - 1, -2, jnp.where(mixed_shifts == GROUPS // 2, -1, places)))
    ordered = mixed_shifts[jnp.argsort(priority, stable=True)]
    shifts = ordered[:TILES // CAP]
    tile_ids = jnp.arange(TILES, dtype=jnp.int32)
    owners = jnp.arange(GROUPS, dtype=jnp.int32)
    target = (owners[:, None] + shifts[tile_ids // CAP][None, :]) % GROUPS
    orders = jax.vmap(lambda one_key: jax.random.permutation(one_key, TILES))(jax.random.split(second_key, GROUPS))
    placed = orders[target, jnp.broadcast_to(tile_ids[None, :], target.shape)]
    return (target * TILES + placed).reshape(-1).astype(jnp.int32)


def pair_tables(key):
    first_key, second_key, third_key, fourth_key = jax.random.split(jax.random.fold_in(key, 7), 4)
    half_groups = GROUPS // 2
    joined = jax.random.randint(first_key, (half_groups,), 0, 2)
    forced = jax.random.randint(second_key, (), 0, half_groups)
    joined = joined.at[forced].set(1)
    lengths = jax.random.randint(third_key, (GROUPS,), ROWS // 2, ROWS + 1)
    shared = jax.random.randint(fourth_key, (half_groups,), ROWS // 2, ROWS + 1)
    shared = shared.at[forced].set(ROWS)
    joined_rows = jnp.repeat(joined, 2)
    lengths = jnp.where(joined_rows == 1, jnp.repeat(shared, 2), lengths)
    group_ids = jnp.arange(GROUPS, dtype=jnp.int32)
    mates = jnp.where(joined_rows == 1, jnp.bitwise_xor(group_ids, 1), group_ids)
    return (lengths.astype(jnp.int32), mates.astype(jnp.int32))


def draw_live(key, part):
    return pair_tables(key)[0]


def draw_partner(key, part):
    return pair_tables(key)[1]


def draw_norm_gains(key, part):
    first_key = jax.random.fold_in(jax.random.fold_in(key, 3), 0)
    lower = jnp.exp(jax.random.uniform(first_key, (3, HEAD), jnp.float32, math.log(0.5), math.log(2.0)))
    return lower


def block_levels(rng, dims, pieces, low, largest):
    factor_of = 1.0
    for dim, shards_of in pieces:
        draws = jax.random.uniform(jax.random.fold_in(jax.random.fold_in(rng, 6), dim), (shards_of,), jnp.float32, low / len(pieces), largest / len(pieces))
        factor_of = factor_of * jnp.repeat(jnp.exp(draws), dims[dim] // shards_of).reshape((-1,) + (1,) * (len(dims) - 1 - dim))
    return factor_of


def gaussian(key, dims, scale, limit, shards=(), held_as=jnp.bfloat16):
    entries = jax.random.normal(key, dims, jnp.float32) * scale
    if len(shards) > 0:
        entries = block_levels(key, dims, shards, -0.22, 0.18) * entries
    return jnp.clip(entries, min=-limit, max=limit).astype(held_as)


def setup_inputs(seed: int = 0) -> dict:
    arg_keys = jax.random.split(jax.random.key(seed), 13)
    latents = gaussian(arg_keys[0], (GROUPS * TILES, TILE * CH), 1.0, 6.0, ((0, 16), (1, 2)), jnp.float32)
    tile_slot = draw_tile_slot(jax.random.fold_in(arg_keys[12], 71), 0)
    live = draw_live(jax.random.fold_in(arg_keys[12], 71), 0)
    partner = draw_partner(jax.random.fold_in(arg_keys[12], 71), 0)
    text_states = gaussian(arg_keys[4], (GROUPS, 2, TEXT, D), 1.0, 6.0, ((0, 16),))
    modulation = gaussian(arg_keys[5], (GROUPS, 2, 5, D), 0.5, 3.0, ((0, 16),), jnp.float32)
    w_embed = gaussian(arg_keys[6], (CH, D), CH ** -0.5, 0.75)
    w_qkv = gaussian(arg_keys[7], (D, 3, HEADS * HEAD), D ** -0.5, 0.125, ((2, 2),))
    w_text_kv = gaussian(arg_keys[8], (D, 2, HEADS * HEAD), D ** -0.5, 0.125, ((2, 2),))
    w_out = gaussian(arg_keys[9], (HEADS * HEAD, D), (HEADS * HEAD) ** -0.5, 0.15625, ((0, 2),))
    w_final = gaussian(arg_keys[10], (D, CH), D ** -0.5, 0.125)
    norm_gains = draw_norm_gains(jax.random.fold_in(arg_keys[12], 71), 0)
    return dict(latents=latents, tile_slot=tile_slot, live=live, partner=partner, text_states=text_states, modulation=modulation, w_embed=w_embed, w_qkv=w_qkv, w_text_kv=w_text_kv, w_out=w_out, w_final=w_final, norm_gains=norm_gains)


GUIDE = 3.5
STEP = -0.25
EPS = 1e-06

def layer_norm(inputs):
    centre = lax.optimization_barrier(jnp.mean(inputs, axis=-1, keepdims=True))
    centred = inputs - centre
    spread = lax.optimization_barrier(jnp.mean(centred * centred, axis=-1, keepdims=True))
    return centred * lax.rsqrt(spread + EPS)

def head_norm(inputs, gains):
    square = lax.optimization_barrier(jnp.mean(inputs * inputs, axis=-1, keepdims=True))
    return (inputs * lax.rsqrt(square + EPS) * gains).astype(jnp.bfloat16)

def finish(residue, mixed, adaptive, w_final):
    state = residue + adaptive[:, 2, None, :] * mixed
    final = (layer_norm(state) * (1.0 + adaptive[:, 4, None, :]) + adaptive[:, 3, None, :]).astype(jnp.bfloat16)
    velocity = jnp.einsum('brd,dc->brc', final.astype(jnp.float32), w_final.astype(jnp.float32))
    return velocity[1] + GUIDE * (velocity[0] - velocity[1])

def reference(latents, tile_slot, live, partner, text_states, modulation, w_embed, w_qkv, w_text_kv, w_out, w_final, norm_gains):
    width = HEADS * HEAD
    buffer = jnp.zeros_like(latents).at[tile_slot].set(latents)
    tokens = buffer.reshape(N_GROUPS, ROWS, CH)
    qkv_weight = w_qkv.astype(jnp.float32)
    text_weight = w_text_kv.astype(jnp.float32)
    out_blocks = w_out.astype(jnp.float32).reshape(N_MP, width // N_MP, D)

    def embed(group_index):
        hidden = jnp.dot(tokens[group_index].astype(jnp.bfloat16), w_embed, preferred_element_type=jnp.float32)
        return hidden

    def project(group_index):
        hidden = embed(group_index)
        adaptive = modulation[group_index]
        normed = (layer_norm(hidden)[None] * (1.0 + adaptive[:, 1, None, :]) + adaptive[:, 0, None, :]).astype(jnp.bfloat16)
        projected = jnp.einsum('brd,dcn->brcn', normed.astype(jnp.float32), qkv_weight).reshape(2, ROWS, 3, HEADS, HEAD)
        query = head_norm(projected[:, :, 0], norm_gains[0])
        image_key = head_norm(projected[:, :, 1], norm_gains[1])
        image_value = projected[:, :, 2].astype(jnp.bfloat16)
        return (query, image_key, image_value)
    queries, image_keys, image_values = lax.map(project, jnp.arange(N_GROUPS, dtype=jnp.int32))
    position = jnp.arange(ROWS, dtype=jnp.int32)

    def attend(group_index):
        mate = partner[group_index]
        joined = mate != group_index
        own_len = live[group_index]
        mate_len = jnp.where(joined, live[mate], 0)
        text_proj = jnp.einsum('btd,dcn->btcn', text_states[group_index].astype(jnp.float32), text_weight).reshape(2, TEXT, 2, HEADS, HEAD)
        text_key = head_norm(text_proj[:, :, 0], norm_gains[2])
        text_value = text_proj[:, :, 1].astype(jnp.bfloat16)
        all_keys = jnp.concatenate([text_key, image_keys[group_index], image_keys[mate]], axis=1)
        all_values = jnp.concatenate([text_value, image_values[group_index], image_values[mate]], axis=1)
        usable = jnp.concatenate([jnp.ones((TEXT,), bool), position < own_len, position < mate_len])
        scores = jnp.einsum('bqhe,bkhe->bhqk', queries[group_index].astype(jnp.float32), all_keys.astype(jnp.float32)) * HEAD ** (-0.5)
        scores = jnp.where(usable[None, None, None, :], scores, -1e+30)
        highest = lax.optimization_barrier(jnp.max(scores, axis=-1, keepdims=True))
        raised = jnp.exp(scores - highest)
        summed = lax.optimization_barrier(jnp.sum(raised, axis=-1, keepdims=True))
        weights = (raised / summed).astype(jnp.bfloat16)
        attended = jnp.einsum('bhqk,bkhe->bqhe', weights.astype(jnp.float32), all_values.astype(jnp.float32)).astype(jnp.bfloat16)
        blocks = attended.reshape(2, ROWS, N_MP, width // N_MP).astype(jnp.float32)
        terms = jnp.einsum('brmn,mnd->mbrd', blocks, out_blocks).astype(jnp.bfloat16)
        terms = lax.optimization_barrier(terms).astype(jnp.float32)
        mixed = lax.optimization_barrier(jnp.sum(terms, axis=0))
        hidden = embed(group_index)
        guided = finish(hidden[None], mixed, modulation[group_index], w_final)
        living = (position < own_len)[:, None]
        return tokens[group_index] + STEP * jnp.where(living, guided, 0.0)
    updated = lax.map(attend, jnp.arange(N_GROUPS, dtype=jnp.int32))
    new_buffer = updated.reshape(N_GROUPS * TILES, TILE * CH)
    return new_buffer[tile_slot]
```

```python
import functools

import jax
import jax.numpy as jnp
from jax import lax
from jax.experimental import pallas as pl
from jax.experimental.pallas import tpu as pltpu
from jax.sharding import PartitionSpec as P

HEAD = 64
CH = 64
TILE = 4
LANES = 128
PACK = 16

GUIDE = 3.5
STEP = -0.25
EPS = 1e-06
LOG2E = 1.4426950408889634
DEAD = -1e30

F32 = jnp.float32
BF16 = jnp.bfloat16
VMEM_LIMIT = 56 * 2**20


def round_up(value, step):
    return (value + step - 1) // step * step


def mm(left, right):
    return jnp.dot(left, right, preferred_element_type=F32)


def mm_nt(left, right):
    return lax.dot_general(left, right, (((1,), (1,)), ((), ())), preferred_element_type=F32)


def iota(shape, dim):
    return lax.broadcasted_iota(jnp.int32, shape, dim)


def two_terms(value):
    high = value.astype(BF16)
    return high, (value - high.astype(F32)).astype(BF16)


def one_hot(mask):
    return jnp.where(mask, 1.0, 0.0).astype(BF16)


def spec(space=pltpu.VMEM):
    return pl.BlockSpec(memory_space=space)


def params(**more):
    return pltpu.CompilerParams(vmem_limit_bytes=VMEM_LIMIT, **more)


def own_bucket(slots, tiles):
    target = slots // tiles
    row = target.astype(F32)
    diagonal = iota((tiles, tiles), 0) == iota((tiles, tiles), 1)
    column = jnp.sum(jnp.where(diagonal, row, 0.0), axis=1, keepdims=True)
    earlier = (column == row) & (iota((tiles, tiles), 0) < iota((tiles, tiles), 1))
    rank = jnp.sum(jnp.where(earlier, 1.0, 0.0), axis=0, keepdims=True).astype(jnp.int32)
    return target, rank


def send_kernel(capacity, block, where_ref, slots_ref, latents_ref, out_ref):
    tiles = latents_ref.shape[0]
    groups_n = out_ref.shape[0]
    target, rank = own_bucket(slots_ref[pl.ds(where_ref[0], 1), :], tiles)
    rows = groups_n * block
    bucket = iota((rows, tiles), 0)
    first = target * block + rank
    second = (target ^ 1) * block + capacity + rank
    sender = one_hot((bucket == first) | (bucket == second))
    sent = mm(sender, latents_ref[...].astype(BF16)).astype(BF16).reshape(groups_n, block, -1)
    out_ref[:, 0] = sent
    out_ref[:, 1] = sent


def tables(slots, group, tiles, capacity, block, offset):
    groups_n = slots.shape[0]
    target = slots // tiles
    placed = slots - target * tiles
    mine = target == group
    before = one_hot(iota((tiles, tiles), 0) < iota((tiles, tiles), 1))
    rank = mm(one_hot(mine), before)
    rank = jnp.where(mine, rank, float(capacity))
    columns = groups_n * block
    spread = one_hot(iota((groups_n, columns), 1) // block == iota((groups_n, columns), 0))
    turn = (((0,), (0,)), ((), ()))
    rank_of = lax.dot_general(rank.astype(BF16), spread, turn, preferred_element_type=F32)
    place_of = lax.dot_general(placed.astype(F32).astype(BF16), spread, turn, preferred_element_type=F32)
    level = (iota((tiles, columns), 1) % block - offset).astype(F32)
    hit = (rank_of == level) & (level >= 0.0) & (level < capacity)
    place = jnp.sum(jnp.where(hit, place_of + 1.0, 0.0), axis=0, keepdims=True) - 1.0
    return one_hot(iota((tiles, columns), 0).astype(F32) == place)


def fold_kernel(
    capacity,
    block,
    back,
    where_ref,
    slots_ref,
    embed_ref,
    own_mod_ref,
    mate_mod_ref,
    w_ref,
    own_out,
    mate_out,
    own_bias,
    mate_bias,
    gram_out,
    place_out,
    home_out,
    left,
):
    step = pl.program_id(0)
    depth = embed_ref.shape[1]
    own_rows = 4 * CH

    @pl.when(step == 0)
    def _():
        embed = embed_ref[...].astype(F32)
        centred = embed - jnp.mean(embed, axis=1, keepdims=True)
        for side, mod_ref in ((0, own_mod_ref), (1, mate_mod_ref)):
            base = side * (own_rows + 2 * PACK)
            for branch in range(2):
                scaled = centred * (1.0 + mod_ref[1, branch : branch + 1, :])
                high, low = two_terms(scaled)
                left[pl.ds(base + branch * 2 * CH, CH), :] = high
                left[pl.ds(base + branch * 2 * CH + CH, CH), :] = low
            high, low = two_terms(mod_ref[0])
            shifts = jnp.concatenate([high.astype(F32), low.astype(F32)], axis=0)
            shifts = jnp.concatenate([shifts, jnp.zeros((2 * PACK - 4, depth), F32)], axis=0)
            left[pl.ds(base + own_rows, 2 * PACK), :] = shifts.astype(BF16)
        high, low = two_terms(centred)
        parts = mm_nt(high, high) + (mm_nt(high, low) + mm_nt(low, high))
        parts = parts * (1.0 / depth)
        top, rest = two_terms(parts)
        bottom = (parts - top.astype(F32) - rest.astype(F32)).astype(BF16)
        gram_out[0:CH, :] = top
        gram_out[CH : 2 * CH, :] = rest
        gram_out[2 * CH : 3 * CH, :] = bottom
        gram_out[3 * CH : 4 * CH, :] = jnp.zeros((CH, CH), BF16)
        tiles = slots_ref.shape[1]
        slots = slots_ref[...]
        group = where_ref[0]
        place_out[0:tiles, :] = tables(slots, group, tiles, capacity, block, 0)
        place_out[tiles : 2 * tiles, :] = tables(slots, group ^ 1, tiles, capacity, block, capacity)
        home_out[...] = tables(slots, group, tiles, capacity, back, 0)

    def keep(product, out_ref, bias_ref):
        for branch in range(2):
            base = branch * 2 * CH
            value = product[base : base + CH] + product[base + CH : base + 2 * CH]
            high, low = two_terms(value)
            out_ref[branch, 0:CH, :] = high
            out_ref[branch, CH : 2 * CH, :] = low
        bias = product[own_rows : own_rows + 2] + product[own_rows + 2 : own_rows + 4]
        bias_ref[0:2, :] = bias

    half = own_rows + 2 * PACK

    @pl.when(step == 0)
    def _():
        keep(mm(left[0:half, :], w_ref[0]), own_out, own_bias)

    @pl.when(step > 0)
    def _():
        product = mm(left[...], w_ref[0])
        keep(product[0:half], own_out, own_bias)
        keep(product[half:], mate_out, mate_bias)


def attend_kernel(
    where_ref,
    live_ref,
    partner_ref,
    arrived_ref,
    place_ref,
    gram_ref,
    own_ref,
    mate_ref,
    own_bias_ref,
    mate_bias_ref,
    text_ref,
    gains_ref,
    keep_ref,
    send_ref,
    tokens_ref,
    proj,
    mate_proj,
    keys_bf,
    values_bf,
):
    group, member = where_ref[0], where_ref[1]
    groups_n, _, block, narrow = arrived_ref.shape
    tiles = place_ref.shape[0] // 2
    rows = tiles * TILE
    half_rows = rows // 2
    width = keep_ref.shape[2]
    text = text_ref.shape[2]
    keys_n = keys_bf.shape[0]
    mate = partner_ref[group]
    own_len = live_ref[group]
    mate_len = jnp.where(mate != group, live_ref[mate], 0)

    own_parts, mate_parts = [], []
    for turn in range(2):
        source = member ^ turn
        block_rows = arrived_ref[:, pl.ds(source, 1)].reshape(groups_n * block, narrow)
        found = mm(place_ref[...], block_rows)
        for parts, base in ((own_parts, 0), (mate_parts, tiles)):
            pair = found[base : base + tiles]
            parts.append(jnp.concatenate([pair[:, :CH], pair[:, :CH]], axis=1))
            parts.append(jnp.concatenate([pair[:, CH:], pair[:, CH:]], axis=1))
    own_tokens = jnp.concatenate(own_parts, axis=0)
    mate_tokens = jnp.concatenate(mate_parts, axis=0)
    tokens_ref[...] = own_tokens[:half_rows].astype(BF16)

    def spread_of(tokens):
        narrow_tokens = tokens.astype(BF16)
        image = mm(narrow_tokens, gram_ref[0 : 2 * CH]) + mm(narrow_tokens, gram_ref[2 * CH :])
        variance = jnp.sum(image * tokens[:, :CH], axis=1, keepdims=True)
        return lax.rsqrt(jnp.maximum(variance, 0.0) + EPS)

    own_scale = spread_of(own_tokens)
    mate_scale = spread_of(mate_tokens)
    own_narrow = own_tokens.astype(BF16)
    mate_narrow = mate_tokens.astype(BF16)

    row = iota((rows, 1), 0)
    turn_of = row // half_rows
    inside = row - turn_of * half_rows
    second = inside // tiles
    slot = (inside - second * tiles) * TILE + 2 * (turn_of ^ member) + second
    own_dead = jnp.where(slot < own_len, 0.0, DEAD)
    mate_dead = jnp.where(slot < mate_len, 0.0, DEAD)
    rest = keys_n - 2 * rows
    text_dead = jnp.where(iota((rest, 1), 0) < text, 0.0, DEAD)
    dead = jnp.concatenate([own_dead, mate_dead, text_dead], axis=0)

    lane = iota((1, LANES), 1)
    even = lane < HEAD
    averaging = jnp.where(
        iota((LANES, LANES), 0) // HEAD == iota((LANES, LANES), 1) // HEAD, 1.0 / HEAD, 0.0
    ).astype(BF16)

    def head_norm(value, gains):
        square = mm((value * value).astype(BF16), averaging)
        return value * (lax.rsqrt(square + EPS) * gains)

    values_bf[2 * rows :, :] = jnp.zeros((rest, LANES), BF16)

    for branch in range(2):
        proj[...] = (
            mm(own_narrow, own_ref[branch]) * own_scale + own_bias_ref[branch : branch + 1, :]
        )
        mate_proj[...] = (
            mm(mate_narrow, mate_ref[branch]) * mate_scale + mate_bias_ref[branch : branch + 1, :]
        )
        for pair in range(width // LANES):
            at = pair * LANES
            query = head_norm(proj[:, at : at + LANES], gains_ref[0:1, :] * (LOG2E * HEAD**-0.5))
            keys = jnp.concatenate(
                [
                    head_norm(proj[:, width + at : width + at + LANES], gains_ref[1:2, :]),
                    head_norm(mate_proj[:, at : at + LANES], gains_ref[1:2, :]),
                    head_norm(text_ref[branch, 0, :, at : at + LANES], gains_ref[2:3, :]),
                    jnp.zeros((rest - text, LANES), F32),
                ],
                axis=0,
            )
            values_bf[0:rows, :] = proj[:, 2 * width + at : 2 * width + at + LANES].astype(BF16)
            values_bf[rows : 2 * rows, :] = mate_proj[:, width + at : width + at + LANES].astype(BF16)
            values_bf[2 * rows : 2 * rows + text, :] = text_ref[branch, 1, :, at : at + LANES].astype(BF16)
            values = values_bf[...]
            outs = []
            for side in range(2):
                inside_head = even if side == 0 else jnp.logical_not(even)
                marker = lane == (HEAD if side == 0 else 0)
                one_query = jnp.where(inside_head, query, jnp.where(marker, 1.0, 0.0)).astype(BF16)
                one_keys = jnp.where(inside_head, keys, jnp.where(marker, dead, 0.0)).astype(BF16)
                one_values = jnp.where(inside_head, values, jnp.ones_like(values))
                scores = mm_nt(one_query, one_keys)
                highest = jnp.max(scores, axis=1, keepdims=True)
                weights = jnp.exp2(scores - highest).astype(BF16)
                outs.append(mm(weights, one_values))
            total = jnp.where(even, outs[1], outs[0])
            total = jnp.concatenate([total[:, HEAD:], total[:, :HEAD]], axis=1)
            merged = (jnp.where(even, outs[0], outs[1]) / total).astype(BF16)
            keep_ref[branch, :, at : at + LANES] = merged[:half_rows]
            send_ref[branch, :, at : at + LANES] = merged[half_rows:]


def finish_kernel(
    back,
    where_ref,
    live_ref,
    kept_ref,
    came_ref,
    w_own_ref,
    w_came_ref,
    tokens_ref,
    embed_ref,
    mod_ref,
    w_final_ref,
    home_ref,
    out_ref,
):
    group, member = where_ref[0], where_ref[1]
    half_rows = tokens_ref.shape[0]
    tiles = home_ref.shape[0]
    hidden = mm(tokens_ref[:, :CH], embed_ref[...])
    velocities = []
    for branch in range(2):
        mixed = mm(kept_ref[branch], w_own_ref[...]).astype(BF16).astype(F32) + mm(
            came_ref[branch], w_came_ref[...]
        ).astype(BF16).astype(F32)
        state = hidden + mod_ref[2, branch : branch + 1, :] * mixed
        centred = state - jnp.mean(state, axis=1, keepdims=True)
        spread = jnp.mean(centred * centred, axis=1, keepdims=True)
        normed = centred * lax.rsqrt(spread + EPS)
        final = normed * (1.0 + mod_ref[4, branch : branch + 1, :]) + mod_ref[3, branch : branch + 1, :]
        velocities.append(mm_nt(final.astype(BF16), w_final_ref[...]))
    guided = velocities[1] + GUIDE * (velocities[0] - velocities[1])
    row = iota((half_rows, 1), 0)
    second = row // tiles
    slot = (row - second * tiles) * TILE + 2 * member + second
    guided = jnp.where(slot < live_ref[group], guided, 0.0)
    columns = jnp.concatenate([guided[:tiles], guided[tiles:]], axis=1).astype(BF16)
    out_ref[...] = lax.dot_general(
        home_ref[...], columns, (((0,), (0,)), ((), ())), preferred_element_type=F32
    ).astype(BF16)


def update_kernel(back, where_ref, slots_ref, latents_ref, returned_ref, out_ref):
    tiles = latents_ref.shape[0]
    target, rank = own_bucket(slots_ref[pl.ds(where_ref[0], 1), :], tiles)
    sender = one_hot(iota((returned_ref.shape[0], tiles), 0) == target * back + rank)
    guided = lax.dot_general(
        sender, returned_ref[...], (((0,), (0,)), ((), ())), preferred_element_type=F32
    )
    out_ref[...] = latents_ref[...] + STEP * guided


def shards(
    latents,
    tile_slot,
    live,
    partner,
    text_states,
    modulation,
    w_embed,
    w_qkv,
    w_text_kv,
    w_out,
    w_final,
    norm_gains,
):
    groups_n = lax.axis_size("groups")
    group = lax.axis_index("groups").astype(jnp.int32)
    member = lax.axis_index("mp").astype(jnp.int32)
    tiles, narrow = latents.shape
    rows = tiles * TILE
    depth = w_embed.shape[1]
    width = w_out.shape[0]
    text = text_states.shape[2]
    capacity = max(2, (tiles + groups_n - 1) // groups_n)
    block = round_up(2 * capacity, PACK)
    back = round_up(capacity, PACK)
    where = jnp.stack([group, member])
    slots = tile_slot.reshape(groups_n, tiles)
    both = ("groups", "mp")

    outbound = pl.pallas_call(
        functools.partial(send_kernel, capacity, block),
        out_shape=jax.ShapeDtypeStruct((groups_n, 2, block, narrow), BF16),
        in_specs=[spec(pltpu.SMEM), spec(), spec()],
        out_specs=spec(),
        compiler_params=params(),
    )(where, slots, latents)
    arrived = lax.all_to_all(
        outbound.reshape(groups_n * 2, block, narrow), both, split_axis=0, concat_axis=0, tiled=True
    ).reshape(groups_n, 2, block, narrow)

    adaptive = jnp.swapaxes(modulation[0], 0, 1)
    pairs = [(source, source ^ 1) for source in range(groups_n)]
    mate_mod = lax.ppermute(adaptive[:2], "groups", pairs)
    came_w_out = lax.ppermute(w_out, "mp", [(0, 1), (1, 0)])

    text_proj = jnp.einsum(
        "btd,dcn->bctn", text_states[0], w_text_kv, preferred_element_type=F32
    )

    left_rows = 2 * (4 * CH + 2 * PACK)
    constant2 = lambda i: (0, 0)
    constant3 = lambda i: (0, 0, 0)
    later = lambda i: jnp.maximum(i - 1, 0)
    own_fold, mate_fold, own_bias, mate_bias, gram, place, home = pl.pallas_call(
        functools.partial(fold_kernel, capacity, block, back),
        grid=(3,),
        out_shape=[
            jax.ShapeDtypeStruct((2, 2 * CH, 3 * width), BF16),
            jax.ShapeDtypeStruct((2, 2 * CH, 2 * width), BF16),
            jax.ShapeDtypeStruct((8, 3 * width), F32),
            jax.ShapeDtypeStruct((8, 2 * width), F32),
            jax.ShapeDtypeStruct((4 * CH, CH), BF16),
            jax.ShapeDtypeStruct((2 * tiles, groups_n * block), BF16),
            jax.ShapeDtypeStruct((tiles, groups_n * back), BF16),
        ],
        in_specs=[
            spec(pltpu.SMEM),
            pl.BlockSpec((groups_n, tiles), constant2),
            pl.BlockSpec((CH, depth), constant2),
            pl.BlockSpec((5, 2, depth), constant3),
            pl.BlockSpec((2, 2, depth), constant3),
            pl.BlockSpec((1, depth, width), lambda i: (i, 0, 0)),
        ],
        out_specs=[
            pl.BlockSpec((2, 2 * CH, width), lambda i: (0, 0, i)),
            pl.BlockSpec((2, 2 * CH, width), lambda i: (0, 0, later(i))),
            pl.BlockSpec((8, width), lambda i: (0, i)),
            pl.BlockSpec((8, width), lambda i: (0, later(i))),
            pl.BlockSpec((4 * CH, CH), constant2),
            pl.BlockSpec((2 * tiles, groups_n * block), constant2),
            pl.BlockSpec((tiles, groups_n * back), constant2),
        ],
        scratch_shapes=[pltpu.VMEM((left_rows, depth), BF16)],
        compiler_params=params(),
        cost_estimate=pl.CostEstimate(
            flops=2 * left_rows * depth * 3 * width, bytes_accessed=2 * depth * 3 * width, transcendentals=0
        ),
    )(where, slots, w_embed, adaptive, mate_mod, jnp.swapaxes(w_qkv, 0, 1))

    gains = jnp.concatenate([norm_gains, norm_gains], axis=1)
    keys_n = round_up(2 * rows + text, LANES)
    half = jax.ShapeDtypeStruct((2, rows // 2, width), BF16)
    kept, sent, tokens = pl.pallas_call(
        attend_kernel,
        out_shape=[half, half, jax.ShapeDtypeStruct((rows // 2, 2 * CH), BF16)],
        in_specs=[spec(pltpu.SMEM)] * 3 + [spec()] * 9,
        out_specs=[spec()] * 3,
        scratch_shapes=[
            pltpu.VMEM((rows, 3 * width), F32),
            pltpu.VMEM((rows, 2 * width), F32),
            pltpu.VMEM((keys_n, LANES), BF16),
            pltpu.VMEM((keys_n, LANES), BF16),
        ],
        compiler_params=params(),
    )(
        where,
        live,
        partner,
        arrived,
        place,
        gram,
        own_fold,
        mate_fold,
        own_bias,
        mate_bias,
        text_proj,
        gains,
    )
    came = lax.ppermute(sent, "mp", [(0, 1), (1, 0)])

    homeward = pl.pallas_call(
        functools.partial(finish_kernel, back),
        out_shape=jax.ShapeDtypeStruct((groups_n * back, narrow), BF16),
        in_specs=[spec(pltpu.SMEM)] * 2 + [spec()] * 9,
        out_specs=spec(),
        compiler_params=params(),
    )(where, live, kept, came, w_out, came_w_out, tokens, w_embed, adaptive, w_final.T, home)
    returned = lax.all_to_all(
        homeward.reshape(groups_n, back, narrow), "groups", split_axis=0, concat_axis=0, tiled=True
    ).reshape(groups_n * back, narrow)
    return pl.pallas_call(
        functools.partial(update_kernel, back),
        out_shape=jax.ShapeDtypeStruct((tiles, narrow), F32),
        in_specs=[spec(pltpu.SMEM)] + [spec()] * 3,
        out_specs=spec(),
        compiler_params=params(),
    )(where, slots, latents, returned)


def solution(mesh):
    placed = (
        P("groups", "mp"),
        P(),
        P(),
        P(),
        P("groups", None, None, None),
        P("groups", None, None, None),
        P(),
        P(None, None, "mp"),
        P(None, None, "mp"),
        P("mp", None),
        P(),
        P(),
    )
    return jax.shard_map(
        shards, mesh=mesh, in_specs=placed, out_specs=P("groups", "mp"), check_vma=False
    )
```

```python
import functools
import math

import jax
import jax.numpy as jnp
from jax import lax
from jax.experimental import pallas as pl
from jax.experimental.pallas import tpu as pltpu
from jax.sharding import PartitionSpec as P

HEAD = 64
CH = 64
TILE = 4
LANES = 128
PACK = 16

GUIDE = 3.5
STEP = -0.25
EPS = 1e-06
LOG2E = 1.4426950408889634
DEAD = -1e30
SEND_MIB, PREPARE_MIB, ATTEND_MIB, FINISH_MIB = 16, 56, 40, 24

F32 = jnp.float32
BF16 = jnp.bfloat16
MIB = 2**20


def round_up(value, step):
    return (value + step - 1) // step * step


def spans(total, step):
    return [(start, min(start + step, total)) for start in range(0, total, step)]


def mm(left, right):
    return jnp.dot(left, right, preferred_element_type=F32)


def mm_nt(left, right):
    return lax.dot_general(left, right, (((1,), (1,)), ((), ())), preferred_element_type=F32)


def mm_tn(left, right):
    return lax.dot_general(left, right, (((0,), (0,)), ((), ())), preferred_element_type=F32)


def iota(shape, dim):
    return lax.broadcasted_iota(jnp.int32, shape, dim)


def two_terms(value):
    high = value.astype(BF16)
    return high, (value - high.astype(F32)).astype(BF16)


def one_hot(mask):
    return jnp.where(mask, 1.0, 0.0).astype(BF16)


def spec(space=pltpu.VMEM):
    return pl.BlockSpec(memory_space=space)


def grant(mib):
    return pltpu.CompilerParams(vmem_limit_bytes=mib * MIB)


def position():
    return lax.axis_index("groups").astype(jnp.int32), lax.axis_index("mp").astype(jnp.int32)


def head_norm(value, gains):
    wide = value.shape[1]
    same = iota((wide, wide), 0) // HEAD == iota((wide, wide), 1) // HEAD
    averaging = jnp.where(same, 1.0 / HEAD, 0.0).astype(BF16)
    square = mm((value * value).astype(BF16), averaging)
    return value * (lax.rsqrt(square + EPS) * gains)


def lanes_of(gains, wide):
    return jnp.concatenate([gains] * (wide // HEAD), axis=1)


def column_of(gains_ref, index):
    row = jnp.broadcast_to(gains_ref[index : index + 1, :], (LANES, HEAD))
    return row.T[:, 0:1]


def head_norm_down(value, gains):
    parts = []
    for at in range(0, value.shape[0], HEAD):
        head = value[at : at + HEAD]
        square = jnp.sum(head * head, axis=0, keepdims=True) * (1.0 / HEAD)
        parts.append(head * lax.rsqrt(square + EPS) * gains)
    return jnp.concatenate(parts, axis=0)


def own_bucket(slots_ref, group, tiles):
    first = group * tiles
    row = first // LANES
    after = jnp.minimum(row + 1, slots_ref.shape[0] - 1)
    window = jnp.concatenate([slots_ref[pl.ds(row, 1), :], slots_ref[pl.ds(after, 1), :]], axis=1)
    turn = 2 * LANES - (first - row * LANES)
    slots = pltpu.roll(window, turn, 1)[:, :tiles]
    target = slots // tiles
    across = target.astype(F32)
    diagonal = iota((tiles, tiles), 0) == iota((tiles, tiles), 1)
    down = jnp.sum(jnp.where(diagonal, across, 0.0), axis=1, keepdims=True)
    earlier = (down == across) & (iota((tiles, tiles), 0) < iota((tiles, tiles), 1))
    rank = jnp.sum(jnp.where(earlier, 1.0, 0.0), axis=0, keepdims=True).astype(jnp.int32)
    return target, rank


def send_kernel(capacity, block, slots_ref, latents_ref, out_ref):
    tiles = latents_ref.shape[0]
    groups_n = out_ref.shape[0]
    group, _ = position()
    target, rank = own_bucket(slots_ref, group, tiles)
    rows = groups_n * block
    bucket = iota((rows, tiles), 0)
    first = target * block + rank
    second = (target ^ 1) * block + capacity + rank
    sender = one_hot((bucket == first) | (bucket == second))
    sent = mm(sender, latents_ref[...].astype(BF16)).astype(BF16).reshape(groups_n, block, -1)
    out_ref[:, 0] = sent
    out_ref[:, 1] = sent


def slots_by_group(slots_ref, tiles):
    per = LANES // math.gcd(tiles, LANES)
    rows_per = per * tiles // LANES
    repeats = slots_ref.shape[0] // rows_per
    wide = jnp.concatenate(
        [slots_ref[pl.ds(row, repeats, stride=rows_per), :] for row in range(rows_per)], axis=1
    )
    parts = [wide[:, turn * tiles : (turn + 1) * tiles] for turn in range(per)]
    return jnp.concatenate(parts, axis=0), lambda row: per * (row % repeats) + row // repeats


def tables(slots, group_of, group, capacity, block, offset):
    groups_n, tiles = slots.shape
    target = slots // tiles
    placed = slots - target * tiles
    mine = target == group
    before = one_hot(iota((tiles, tiles), 0) < iota((tiles, tiles), 1))
    rank = jnp.where(mine, mm(one_hot(mine), before), float(capacity))
    columns = groups_n * block
    spread = one_hot(iota((groups_n, columns), 1) // block == group_of(iota((groups_n, columns), 0)))
    rank_of = mm_tn(rank.astype(BF16), spread)
    place_of = mm_tn(placed.astype(F32).astype(BF16), spread)
    level = (iota((tiles, columns), 1) % block - offset).astype(F32)
    hit = (rank_of == level) & (level >= 0.0) & (level < capacity)
    place = jnp.sum(jnp.where(hit, place_of + 1.0, 0.0), axis=0, keepdims=True) - 1.0
    return one_hot(iota((tiles, columns), 0).astype(F32) == place)


def prepare_kernel(
    capacity,
    block,
    back,
    step,
    slots_ref,
    embed_ref,
    own_mod_ref,
    mate_mod_ref,
    gains_ref,
    states_hbm,
    w_text_hbm,
    w_qkv_hbm,
    gram_out,
    place_out,
    home_out,
    folds_out,
    turned_out,
    text_keys_out,
    text_values_out,
    states,
    w_text,
    w_qkv,
    flat,
    mingled,
    wide,
    split,
    sums,
    left,
    sems,
):
    depth = embed_ref.shape[1]
    width = w_qkv.shape[2]
    text = states.shape[0]
    tiles = home_out.shape[0]
    group, _ = position()
    own_rows = 2 * CH
    half = own_rows + PACK
    chunks = spans(depth, step)
    lane_tiles = width // LANES

    def fetch(source, target, index):
        copy = pltpu.make_async_copy(source, target, sems.at[index])
        copy.start()
        return copy

    states_copy = fetch(states_hbm, states, 0)
    text_copies = [
        fetch(w_text_hbm.at[pl.ds(low, high - low)], w_text.at[pl.ds(low, high - low)], 1 + turn)
        for turn, (low, high) in enumerate(chunks)
    ]
    qkv_copies = [
        fetch(w_qkv_hbm.at[part], w_qkv.at[part], 1 + len(chunks) + part) for part in range(3)
    ]

    embed = embed_ref[...].astype(F32)
    centred = embed - jnp.mean(embed, axis=1, keepdims=True)
    for side, mod_ref in ((0, own_mod_ref), (1, mate_mod_ref)):
        base = side * half
        for branch in range(2):
            scaled = centred * (1.0 + mod_ref[1, branch : branch + 1, :])
            left[pl.ds(base + branch * CH, CH), :] = scaled.astype(BF16)
        high, low = two_terms(mod_ref[0])
        shifts = jnp.concatenate([high.astype(F32), low.astype(F32)], axis=0)
        shifts = jnp.concatenate([shifts, jnp.zeros((PACK - 4, depth), F32)], axis=0)
        left[pl.ds(base + own_rows, PACK), :] = shifts.astype(BF16)
    high, low = two_terms(centred)
    parts = (mm_nt(high, high) + (mm_nt(high, low) + mm_nt(low, high))) * (1.0 / depth)
    top, rest = two_terms(parts)
    bottom = (parts - top.astype(F32) - rest.astype(F32)).astype(BF16)
    gram_out[0:CH, :] = top
    gram_out[CH : 2 * CH, :] = rest
    gram_out[2 * CH : 3 * CH, :] = bottom
    gram_out[3 * CH : 4 * CH, :] = jnp.zeros((CH, CH), BF16)
    slots, group_of = slots_by_group(slots_ref, tiles)
    place_out[0:tiles, :] = tables(slots, group_of, group, capacity, block, 0)
    place_out[tiles : 2 * tiles, :] = tables(slots, group_of, group ^ 1, capacity, block, capacity)
    home_out[...] = tables(slots, group_of, group, capacity, back, 0)

    states_copy.wait()
    flat[...] = states[...].reshape(2 * text, depth)
    for turn, (low, high) in enumerate(chunks):
        text_copies[turn].wait()
        count = high - low
        mingled[0 : 2 * count, :] = w_text[low:high].reshape(2 * count, width)
        for index in range(lane_tiles):
            lanes = slice(index * LANES, (index + 1) * LANES)
            wide[index, 0 : 2 * count, :] = mingled[0 : 2 * count, lanes].astype(F32)
        for part in range(2):
            for index in range(lane_tiles):
                lanes = slice(part * width + index * LANES, part * width + (index + 1) * LANES)
                split[low:high, lanes] = wide[index, pl.ds(part, count, stride=2), :].astype(BF16)
    product = mm(flat[...], split[...])
    for index in range(2 * lane_tiles):
        sums[index] = product[:, index * LANES : (index + 1) * LANES]
    rest_rows = text_values_out.shape[1] - text
    padding = jnp.zeros((rest_rows, LANES), F32)
    gains = column_of(gains_ref, 2)
    for branch in range(2):
        for index in range(lane_tiles):
            lanes = slice(index * LANES, (index + 1) * LANES)
            rows = pl.ds(branch, text, stride=2)
            keys = jnp.concatenate([sums[index, rows, :], padding], axis=0).T
            text_keys_out[branch, lanes, :] = head_norm_down(keys, gains).astype(BF16)
            values = jnp.concatenate([sums[lane_tiles + index, rows, :], padding], axis=0)
            text_values_out[branch, :, lanes] = values.astype(BF16)

    def pieces(product, base, branch):
        bias = (
            product[base + own_rows + branch : base + own_rows + branch + 1]
            + product[base + own_rows + 2 + branch : base + own_rows + 3 + branch]
        )
        fold = product[base + branch * CH : base + (branch + 1) * CH]
        high, low = two_terms(fold)
        bias_high, bias_low = two_terms(bias)
        shift = [bias_high.astype(F32), bias_low.astype(F32)]
        return high.astype(F32), low.astype(F32), shift

    def keep(product, base, kind, lanes):
        for branch in range(2):
            high, low, shift = pieces(product, base, branch)
            zeros = jnp.zeros((PACK - 2, high.shape[1]), F32)
            stacked = jnp.concatenate([high, low] + shift + [zeros], axis=0)
            folds_out[branch, kind, :, lanes] = stacked.astype(BF16)

    def keep_turned(product, base, side, lanes):
        for branch in range(2):
            high, low, shift = pieces(product, base, branch)
            zeros = jnp.zeros((CH - 2, high.shape[1]), F32)
            stacked = jnp.concatenate([high, low, high] + shift + [zeros], axis=0)
            turned_out[branch, side, lanes, :] = stacked.T.astype(BF16)

    shared = width // (2 * LANES) * (2 * LANES)
    main, edge = slice(0, shared), slice(shared, width)
    qkv_copies[0].wait()
    keep(mm(left[0:half, :], w_qkv[0]), 0, 0, slice(0, width))
    qkv_copies[1].wait()
    product = mm(left[...], w_qkv[1, :, main])
    keep_turned(product, 0, 0, main)
    keep_turned(product, half, 1, main)
    qkv_copies[2].wait()
    product = mm(left[...], w_qkv[2, :, main])
    keep(product, 0, 1, main)
    keep(product, half, 2, main)
    if shared < width:
        edges = jnp.concatenate([w_qkv[1, :, edge], w_qkv[2, :, edge]], axis=1)
        product = mm(left[...], edges)
        keys, values = product[:, : width - shared], product[:, width - shared :]
        keep_turned(keys, 0, 0, edge)
        keep_turned(keys, half, 1, edge)
        keep(values, 0, 1, edge)
        keep(values, half, 2, edge)


def attend_kernel(
    live_ref,
    partner_ref,
    arrived_ref,
    place_ref,
    gram_ref,
    gains_ref,
    folds_ref,
    turned_ref,
    text_keys_ref,
    text_values_ref,
    keep_ref,
    send_ref,
    tokens_ref,
    queries,
    keys,
    values,
    *,
    text,
):
    group, member = position()
    groups_n, _, block, narrow = arrived_ref.shape
    tiles = place_ref.shape[0] // 2
    rows = tiles * TILE
    half_rows = rows // 2
    width = keep_ref.shape[2]
    rest = text_values_ref.shape[1]
    mate = partner_ref[group]
    own_len = live_ref[group]
    mate_len = jnp.where(mate != group, live_ref[mate], 0)

    own_parts, mate_parts = [], []
    for turn in range(2):
        source = member ^ turn
        block_rows = arrived_ref[:, pl.ds(source, 1)].reshape(groups_n * block, narrow)
        found = mm(place_ref[...], block_rows)
        for parts, base in ((own_parts, 0), (mate_parts, tiles)):
            pair = found[base : base + tiles]
            parts.append(jnp.concatenate([pair[:, :CH], pair[:, :CH]], axis=1))
            parts.append(jnp.concatenate([pair[:, CH:], pair[:, CH:]], axis=1))
    own_tokens = jnp.concatenate(own_parts, axis=0)
    mate_tokens = jnp.concatenate(mate_parts, axis=0)
    tokens_ref[...] = own_tokens[:half_rows].astype(BF16)
    lane = iota((1, LANES), 1)

    def normed(tokens):
        narrow_tokens = tokens.astype(BF16)
        image = mm(narrow_tokens, gram_ref[0 : 2 * CH]) + mm(narrow_tokens, gram_ref[2 * CH :])
        variance = jnp.sum(image * tokens[:, :CH], axis=1, keepdims=True)
        scaled = tokens * lax.rsqrt(jnp.maximum(variance, 0.0) + EPS)
        high = scaled.astype(BF16).astype(F32)
        ones = jnp.where(lane < CH + 2, 1.0, 0.0)
        return jnp.concatenate([high, jnp.where(lane < CH, scaled - high, ones)], axis=1)

    own_normed = normed(own_tokens)
    mate_normed = normed(mate_tokens)
    own_turned = own_normed.T.astype(BF16)
    mate_turned = mate_normed.T.astype(BF16)
    own_normed = own_normed.astype(BF16)
    mate_normed = mate_normed.astype(BF16)

    row = iota((1, rows), 1)
    turn_of = row // half_rows
    inside = row - turn_of * half_rows
    second = inside // tiles
    slot = (inside - second * tiles) * TILE + 2 * (turn_of ^ member) + second
    own_dead = jnp.where(slot < own_len, 0.0, DEAD)
    mate_dead = jnp.where(slot < mate_len, 0.0, DEAD)
    text_dead = jnp.where(iota((1, rest), 1) < text, 0.0, DEAD)
    dead = jnp.concatenate([own_dead, mate_dead, text_dead], axis=1)
    dead = jnp.where(iota((PACK, 1), 0) == 0, dead, 0.0).astype(BF16)
    dead = jnp.concatenate([dead, jnp.zeros((HEAD - PACK, dead.shape[1]), BF16)], axis=0)

    even = lane < HEAD
    query_gains = gains_ref[0:1, :] * (LOG2E * HEAD**-0.5)
    key_gains = column_of(gains_ref, 1)
    filling = jnp.zeros((CH - PACK, width), BF16)

    def fold_of(branch, kind):
        fold = folds_ref[branch, kind]
        return jnp.concatenate([fold[: 2 * CH], fold[:CH], fold[2 * CH :], filling], axis=0)

    def project(branch):
        queries[branch] = mm(own_normed, fold_of(branch, 0))
        values[branch, 0:rows, :] = mm(own_normed, fold_of(branch, 1)).astype(BF16)
        values[branch, rows : 2 * rows, :] = mm(mate_normed, fold_of(branch, 2)).astype(BF16)
        values[branch, 2 * rows :, :] = text_values_ref[branch]
        for side, turned in ((0, own_turned), (1, mate_turned)):
            found = mm(turned_ref[branch, side], turned)
            keys[branch, :, side * rows : (side + 1) * rows] = head_norm_down(found, key_gains).astype(BF16)
        keys[branch, :, 2 * rows :] = text_keys_ref[branch]

    outs = []

    def settle(branch, at, side, one_values, scores):
        highest = jnp.max(scores, axis=1, keepdims=True)
        outs.append(mm(jnp.exp2(scores - highest).astype(BF16), one_values))
        if side == 1:
            first, second = outs
            outs.clear()
            total = jnp.where(even, second, first)
            total = jnp.concatenate([total[:, HEAD:], total[:, :HEAD]], axis=1)
            merged = (jnp.where(even, first, second) / total).astype(BF16)
            keep_ref[branch, :, at : at + LANES] = merged[:half_rows]
            send_ref[branch, :, at : at + LANES] = merged[half_rows:]

    waiting = None
    for branch in range(2):
        project(branch)
        for low, high in spans(width, 2 * LANES):
            normed_queries = head_norm(queries[branch, :, low:high], lanes_of(query_gains, high - low))
            for at in range(low, high, LANES):
                query = normed_queries[:, at - low : at - low + LANES]
                for side in range(2):
                    inside_head = even if side == 0 else jnp.logical_not(even)
                    marker = lane == (HEAD if side == 0 else 0)
                    one_query = jnp.where(inside_head, query, jnp.where(marker, 1.0, 0.0)).astype(BF16)
                    first = at + side * HEAD
                    one_keys = keys[branch, first : first + HEAD, :]
                    one_keys = jnp.concatenate([one_keys, dead] if side == 0 else [dead, one_keys], axis=0)
                    scores = mm(one_query, one_keys)
                    if waiting is not None:
                        settle(*waiting)
                    one_values = values[branch, :, at : at + LANES]
                    one_values = jnp.where(inside_head, one_values, jnp.ones_like(one_values))
                    waiting = (branch, at, side, one_values, scores)
    settle(*waiting)


def finish_kernel(
    step,
    live_ref,
    kept_ref,
    came_ref,
    w_own_ref,
    w_came_ref,
    tokens_ref,
    embed_ref,
    mod_ref,
    w_final_ref,
    home_ref,
    out_ref,
    state,
):
    group, member = position()
    half_rows = tokens_ref.shape[0]
    tiles = home_ref.shape[0]
    width, depth = w_own_ref.shape
    both = 2 * half_rows
    kept = kept_ref[...].reshape(both, width)
    came = came_ref[...].reshape(both, width)
    chunks = spans(depth, step)

    def rows_of(index, low, high):
        first = jnp.broadcast_to(mod_ref[index, 0:1, low:high], (half_rows, high - low))
        second = jnp.broadcast_to(mod_ref[index, 1:2, low:high], (half_rows, high - low))
        return jnp.concatenate([first, second], axis=0)

    def folded(value):
        return sum(value[:, at : at + LANES] for at in range(0, value.shape[1], LANES))

    pivot = None
    total = jnp.zeros((both, LANES), F32)
    squares = jnp.zeros((both, LANES), F32)
    for low, high in chunks:
        mixed = mm(kept, w_own_ref[:, low:high]).astype(BF16).astype(F32) + mm(
            came, w_came_ref[:, low:high]
        ).astype(BF16).astype(F32)
        hidden = mm(tokens_ref[:, :CH], embed_ref[:, low:high])
        hidden = jnp.concatenate([hidden, hidden], axis=0)
        value = hidden + rows_of(2, low, high) * mixed
        if pivot is None:
            pivot = jnp.sum(folded(value), axis=1, keepdims=True) * (1.0 / (high - low))
        value = value - pivot
        state[:, low:high] = value
        total += folded(value)
        squares += folded(value * value)
    mean = jnp.sum(total, axis=1, keepdims=True) * (1.0 / depth)
    spread = jnp.sum(squares, axis=1, keepdims=True) * (1.0 / depth) - mean * mean
    scale = lax.rsqrt(jnp.maximum(spread, 0.0) + EPS)
    offset = -mean * scale
    velocity = jnp.zeros((both, CH), F32)
    for low, high in chunks:
        normed = state[:, low:high] * scale + offset
        final = normed * (1.0 + rows_of(4, low, high)) + rows_of(3, low, high)
        velocity += mm_nt(final.astype(BF16), w_final_ref[:, low:high])
    guided = velocity[half_rows:] + GUIDE * (velocity[:half_rows] - velocity[half_rows:])
    row = iota((half_rows, 1), 0)
    second = row // tiles
    slot = (row - second * tiles) * TILE + 2 * member + second
    guided = jnp.where(slot < live_ref[group], guided, 0.0)
    columns = jnp.concatenate([guided[:tiles], guided[tiles:]], axis=1).astype(BF16)
    out_ref[...] = mm_tn(home_ref[...], columns).astype(BF16)


def update_kernel(back, slots_ref, latents_ref, returned_ref, out_ref):
    tiles = latents_ref.shape[0]
    group, _ = position()
    target, rank = own_bucket(slots_ref, group, tiles)
    sender = one_hot(iota((returned_ref.shape[0], tiles), 0) == target * back + rank)
    out_ref[...] = latents_ref[...] + STEP * mm_tn(sender, returned_ref[...])


def shards(
    latents,
    tile_slot,
    live,
    partner,
    text_states,
    modulation,
    w_embed,
    w_qkv,
    w_text_kv,
    w_out,
    w_final,
    norm_gains,
):
    groups_n = lax.axis_size("groups")
    tiles, narrow = latents.shape
    rows = tiles * TILE
    depth = w_embed.shape[1]
    width = w_out.shape[0]
    text = text_states.shape[2]
    capacity = max(2, (tiles + groups_n - 1) // groups_n)
    block = round_up(2 * capacity, PACK)
    back = round_up(capacity, PACK)
    slots = tile_slot.reshape(groups_n * tiles // LANES, LANES)
    both = ("groups", "mp")
    cores = [(0, 1), (1, 0)]

    adaptive = jnp.swapaxes(modulation[0], 0, 1)
    pairs = [(source, source ^ 1) for source in range(groups_n)]
    mate_mod = lax.ppermute(adaptive, "groups", pairs)

    outbound = pl.pallas_call(
        functools.partial(send_kernel, capacity, block),
        out_shape=jax.ShapeDtypeStruct((groups_n, 2, block, narrow), BF16),
        in_specs=[spec(), spec()],
        out_specs=spec(),
        compiler_params=grant(SEND_MIB),
    )(slots, latents)
    arrived = lax.all_to_all(
        outbound.reshape(groups_n * 2, block, narrow), both, split_axis=0, concat_axis=0, tiled=True
    ).reshape(groups_n, 2, block, narrow)

    step = 5 * LANES
    chunk_n = len(spans(depth, step))
    left_rows = 2 * (2 * CH + PACK)
    rest = round_up(2 * rows + text, 2 * LANES) - 2 * rows
    gram, place, home, folds, turned, text_keys, text_values = pl.pallas_call(
        functools.partial(prepare_kernel, capacity, block, back, step),
        out_shape=[
            jax.ShapeDtypeStruct((4 * CH, CH), BF16),
            jax.ShapeDtypeStruct((2 * tiles, groups_n * block), BF16),
            jax.ShapeDtypeStruct((tiles, groups_n * back), BF16),
            jax.ShapeDtypeStruct((2, 3, 2 * CH + PACK, width), BF16),
            jax.ShapeDtypeStruct((2, 2, width, 4 * CH), BF16),
            jax.ShapeDtypeStruct((2, width, rest), BF16),
            jax.ShapeDtypeStruct((2, rest, width), BF16),
        ],
        in_specs=[spec()] * 5 + [spec(pltpu.HBM)] * 3,
        out_specs=[spec()] * 7,
        scratch_shapes=[
            pltpu.VMEM((text, 2, depth), BF16),
            pltpu.VMEM((depth, 2, width), BF16),
            pltpu.VMEM((3, depth, width), BF16),
            pltpu.VMEM((2 * text, depth), BF16),
            pltpu.VMEM((2 * step, width), BF16),
            pltpu.VMEM((width // LANES, 2 * step, LANES), F32),
            pltpu.VMEM((depth, 2 * width), BF16),
            pltpu.VMEM((2 * width // LANES, 2 * text, LANES), F32),
            pltpu.VMEM((left_rows, depth), BF16),
            pltpu.SemaphoreType.DMA((1 + chunk_n + 3,)),
        ],
        compiler_params=grant(PREPARE_MIB),
        cost_estimate=pl.CostEstimate(
            flops=2 * (left_rows * 3 + 4 * text) * depth * width,
            bytes_accessed=2 * depth * 5 * width,
            transcendentals=0,
        ),
    )(
        slots,
        w_embed,
        adaptive,
        mate_mod,
        norm_gains,
        jnp.swapaxes(text_states[0], 0, 1),
        w_text_kv,
        jnp.swapaxes(w_qkv, 0, 1),
    )

    _, w_out_sent = lax.optimization_barrier((gram, w_out))
    came_w_out = lax.ppermute(w_out_sent, "mp", cores)
    half = jax.ShapeDtypeStruct((2, rows // 2, width), BF16)
    kept, sent, tokens = pl.pallas_call(
        functools.partial(attend_kernel, text=text),
        out_shape=[half, half, jax.ShapeDtypeStruct((rows // 2, 2 * CH), BF16)],
        in_specs=[spec(pltpu.SMEM)] * 2 + [spec()] * 8,
        out_specs=[spec()] * 3,
        scratch_shapes=[
            pltpu.VMEM((2, rows, width), F32),
            pltpu.VMEM((2, width, 2 * rows + rest), BF16),
            pltpu.VMEM((2, 2 * rows + rest, width), BF16),
        ],
        compiler_params=grant(ATTEND_MIB),
        cost_estimate=pl.CostEstimate(
            flops=2 * 2 * 2 * rows * (2 * rows + rest) * width * 4,
            bytes_accessed=8 * MIB,
            transcendentals=0,
        ),
    )(live, partner, arrived, place, gram, norm_gains, folds, turned, text_keys, text_values)
    came = lax.ppermute(sent, "mp", cores)

    homeward = pl.pallas_call(
        functools.partial(finish_kernel, 4 * LANES),
        out_shape=jax.ShapeDtypeStruct((groups_n * back, narrow), BF16),
        in_specs=[spec(pltpu.SMEM)] + [spec()] * 9,
        out_specs=spec(),
        scratch_shapes=[pltpu.VMEM((rows, depth), F32)],
        compiler_params=grant(FINISH_MIB),
    )(live, kept, came, w_out, came_w_out, tokens, w_embed, adaptive, w_final.T, home)
    returned = lax.all_to_all(
        homeward.reshape(groups_n, back, narrow), "groups", split_axis=0, concat_axis=0, tiled=True
    ).reshape(groups_n * back, narrow)
    return pl.pallas_call(
        functools.partial(update_kernel, back),
        out_shape=jax.ShapeDtypeStruct((tiles, narrow), F32),
        in_specs=[spec()] * 3,
        out_specs=spec(),
        compiler_params=grant(SEND_MIB),
    )(slots, latents, returned)


def solution(mesh):
    placed = (
        P("groups", "mp"),
        P(),
        P(),
        P(),
        P("groups", None, None, None),
        P("groups", None, None, None),
        P(),
        P(None, None, "mp"),
        P(None, None, "mp"),
        P("mp", None),
        P(),
        P(),
    )
    return jax.shard_map(
        shards, mesh=mesh, in_specs=placed, out_specs=P("groups", "mp"), check_vma=False
    )
```

```python
import functools
import math

import jax
import jax.numpy as jnp
from jax import lax
from jax.experimental import pallas as pl
from jax.experimental.pallas import tpu as pltpu
from jax.sharding import PartitionSpec as P

HEAD = 64
CH = 64
TILE = 4
LANES = 128
PACK = 16

GUIDE = 3.5
STEP = -0.25
EPS = 1e-06
LOG2E = 1.4426950408889634
DEAD = -1e30
SEND_MIB, PREPARE_MIB, ATTEND_MIB, FINISH_MIB, UPDATE_MIB = 60, 56, 52, 24, 16
AHEAD = 99

F32 = jnp.float32
BF16 = jnp.bfloat16
MIB = 2**20


def round_up(value, step):
    return (value + step - 1) // step * step


def spans(total, step):
    return [(start, min(start + step, total)) for start in range(0, total, step)]


def mm(left, right):
    return jnp.dot(left, right, preferred_element_type=F32)


def mm_nt(left, right):
    return lax.dot_general(left, right, (((1,), (1,)), ((), ())), preferred_element_type=F32)


def mm_tn(left, right):
    return lax.dot_general(left, right, (((0,), (0,)), ((), ())), preferred_element_type=F32)


def iota(shape, dim):
    return lax.broadcasted_iota(jnp.int32, shape, dim)


def two_terms(value):
    high = value.astype(BF16)
    return high, (value - high.astype(F32)).astype(BF16)


def one_hot(mask):
    return jnp.where(mask, 1.0, 0.0).astype(BF16)


def spec(space=pltpu.VMEM):
    return pl.BlockSpec(memory_space=space)


def grant(mib):
    return pltpu.CompilerParams(vmem_limit_bytes=mib * MIB)


def position():
    return lax.axis_index("groups").astype(jnp.int32), lax.axis_index("mp").astype(jnp.int32)


def head_norm(value, gains):
    wide = value.shape[1]
    same = iota((wide, wide), 0) // HEAD == iota((wide, wide), 1) // HEAD
    averaging = jnp.where(same, 1.0 / HEAD, 0.0).astype(BF16)
    square = mm((value * value).astype(BF16), averaging)
    return value * (lax.rsqrt(square + EPS) * gains)


def lanes_of(gains, wide):
    return jnp.concatenate([gains] * (wide // HEAD), axis=1)


def column_of(gains_ref, index):
    row = jnp.broadcast_to(gains_ref[index : index + 1, :], (LANES, HEAD))
    return row.T[:, 0:1]


def head_norm_down(value, gains):
    parts = []
    for at in range(0, value.shape[0], HEAD):
        head = value[at : at + HEAD]
        square = jnp.sum(head * head, axis=0, keepdims=True) * (1.0 / HEAD)
        parts.append(head * lax.rsqrt(square + EPS) * gains)
    return jnp.concatenate(parts, axis=0)


def own_bucket(slots_ref, group, tiles):
    first = group * tiles
    row = first // LANES
    after = jnp.minimum(row + 1, slots_ref.shape[0] - 1)
    window = jnp.concatenate([slots_ref[pl.ds(row, 1), :], slots_ref[pl.ds(after, 1), :]], axis=1)
    turn = 2 * LANES - (first - row * LANES)
    slots = pltpu.roll(window, turn, 1)[:, :tiles]
    target = slots // tiles
    across = target.astype(F32)
    diagonal = iota((tiles, tiles), 0) == iota((tiles, tiles), 1)
    down = jnp.sum(jnp.where(diagonal, across, 0.0), axis=1, keepdims=True)
    earlier = (down == across) & (iota((tiles, tiles), 0) < iota((tiles, tiles), 1))
    rank = jnp.sum(jnp.where(earlier, 1.0, 0.0), axis=0, keepdims=True).astype(jnp.int32)
    return target, rank


def send_kernel(capacity, block, slots_ref, latents_ref, out_ref):
    tiles = latents_ref.shape[0]
    groups_n = out_ref.shape[0]
    group, _ = position()
    target, rank = own_bucket(slots_ref, group, tiles)
    rows = groups_n * block
    bucket = iota((rows, tiles), 0)
    first = target * block + rank
    second = (target ^ 1) * block + capacity + rank
    sender = one_hot((bucket == first) | (bucket == second))
    sent = mm(sender, latents_ref[...].astype(BF16)).astype(BF16).reshape(groups_n, block, -1)
    out_ref[:, 0] = sent
    out_ref[:, 1] = sent


def slots_by_group(slots_ref, tiles):
    per = LANES // math.gcd(tiles, LANES)
    rows_per = per * tiles // LANES
    repeats = slots_ref.shape[0] // rows_per
    wide = jnp.concatenate(
        [slots_ref[pl.ds(row, repeats, stride=rows_per), :] for row in range(rows_per)], axis=1
    )
    parts = [wide[:, turn * tiles : (turn + 1) * tiles] for turn in range(per)]
    return jnp.concatenate(parts, axis=0), lambda row: per * (row % repeats) + row // repeats


def tables(slots, group_of, group, capacity, block, offset):
    groups_n, tiles = slots.shape
    target = slots // tiles
    placed = slots - target * tiles
    mine = target == group
    before = one_hot(iota((tiles, tiles), 0) < iota((tiles, tiles), 1))
    rank = jnp.where(mine, mm(one_hot(mine), before), float(capacity))
    columns = groups_n * block
    spread = one_hot(iota((groups_n, columns), 1) // block == group_of(iota((groups_n, columns), 0)))
    rank_of = mm_tn(rank.astype(BF16), spread)
    place_of = mm_tn(placed.astype(F32).astype(BF16), spread)
    level = (iota((tiles, columns), 1) % block - offset).astype(F32)
    hit = (rank_of == level) & (level >= 0.0) & (level < capacity)
    place = jnp.sum(jnp.where(hit, place_of + 1.0, 0.0), axis=0, keepdims=True) - 1.0
    return one_hot(iota((tiles, columns), 0).astype(F32) == place)


def prepare_kernel(
    capacity,
    block,
    back,
    step,
    slots_ref,
    embed_ref,
    own_mod_ref,
    mate_mod_ref,
    gains_ref,
    states_hbm,
    w_text_hbm,
    w_qkv_hbm,
    gram_out,
    place_out,
    home_out,
    folds_hbm,
    turned_hbm,
    text_keys_hbm,
    text_values_hbm,
    folds_out,
    turned_out,
    text_keys_out,
    text_values_out,
    states,
    mingled,
    w_qkv,
    wide,
    split,
    sums,
    left,
    sems,
    out_sems,
):
    depth = embed_ref.shape[1]
    width = w_qkv.shape[2]
    text = states.shape[0]
    tiles = home_out.shape[0]
    group, _ = position()
    own_rows = 2 * CH
    half = own_rows + PACK
    chunks = spans(depth, step)
    lane_tiles = width // LANES

    sources = []
    for part in range(3):
        for low, high in spans(depth, 2 * step):
            rows = pl.ds(low, high - low)
            sources.append((w_qkv_hbm.at[part, rows], w_qkv.at[part, rows]))
    qkv_n = len(sources) // 3
    sources.append((states_hbm, states))
    w_mingled = w_text_hbm.reshape(2 * depth, width)
    for low, high in chunks:
        rows = pl.ds(2 * low, 2 * (high - low))
        sources.append((w_mingled.at[rows], mingled.at[rows]))
    copies = [
        pltpu.make_async_copy(source, target, sems.at[index])
        for index, (source, target) in enumerate(sources)
    ]
    started = [0]

    def start(count):
        while started[0] < min(count, len(copies)):
            copies[started[0]].start()
            started[0] += 1

    def wait(first, last):
        for index in range(first, last):
            start(index + AHEAD)
            copies[index].wait()

    start(AHEAD)

    embed = embed_ref[...].astype(F32)
    centred = embed - jnp.mean(embed, axis=1, keepdims=True)
    for side, mod_ref in ((0, own_mod_ref), (1, mate_mod_ref)):
        base = side * half
        for branch in range(2):
            scaled = centred * (1.0 + mod_ref[1, branch : branch + 1, :])
            left[pl.ds(base + branch * CH, CH), :] = scaled.astype(BF16)
        high, low = two_terms(mod_ref[0])
        shifts = jnp.concatenate([high.astype(F32), low.astype(F32)], axis=0)
        shifts = jnp.concatenate([shifts, jnp.zeros((PACK - 4, depth), F32)], axis=0)
        left[pl.ds(base + own_rows, PACK), :] = shifts.astype(BF16)
    def pieces(product, base, branch):
        first = base + own_rows + branch
        bias = two_terms(product[first : first + 1] + product[first + 2 : first + 3])
        fold = two_terms(product[base + branch * CH : base + (branch + 1) * CH])
        return [part.astype(F32) for part in fold + bias]

    def keep(product, base, side, lanes):
        for branch in range(2):
            zeros = jnp.zeros((PACK - 2, product.shape[1]), F32)
            stacked = jnp.concatenate(pieces(product, base, branch) + [zeros], axis=0)
            folds_out[branch, side, :, lanes] = stacked.astype(BF16)

    def keep_turned(product, base, kind, lanes):
        for branch in range(2):
            high, low, bias_high, bias_low = pieces(product, base, branch)
            zeros = jnp.zeros((CH - 2, product.shape[1]), F32)
            stacked = jnp.concatenate([high, low, high, bias_high, bias_low, zeros], axis=0)
            turned_out[branch, kind, lanes, :] = stacked.T.astype(BF16)

    shared = width // (2 * LANES) * (2 * LANES)
    main, edge = slice(0, shared), slice(shared, width)
    def gram_and_tables():
        high, low = two_terms(centred)
        parts = (mm_nt(high, high) + (mm_nt(high, low) + mm_nt(low, high))) * (1.0 / depth)
        top, rest = two_terms(parts)
        bottom = (parts - top.astype(F32) - rest.astype(F32)).astype(BF16)
        gram_out[0:CH, :] = top
        gram_out[CH : 2 * CH, :] = rest
        gram_out[2 * CH : 3 * CH, :] = bottom
        gram_out[3 * CH : 4 * CH, :] = jnp.zeros((CH, CH), BF16)
        slots, group_of = slots_by_group(slots_ref, tiles)
        place_out[0:tiles, :] = tables(slots, group_of, group, capacity, block, 0)
        place_out[tiles : 2 * tiles, :] = tables(slots, group_of, group ^ 1, capacity, block, capacity)
        home_out[...] = tables(slots, group_of, group, capacity, back, 0)

    out_copies = []

    def put(source, target):
        out_copies.append(pltpu.make_async_copy(source, target, out_sems.at[len(out_copies)]))
        out_copies[-1].start()

    def divide(first, last):
        for low, high in chunks[first:last]:
            count = high - low
            for index in range(lane_tiles):
                lanes = slice(index * LANES, (index + 1) * LANES)
                wide[index, 0 : 2 * count, :] = mingled[2 * low : 2 * high, lanes].astype(F32)
            for part in range(2):
                for index in range(lane_tiles):
                    lanes = slice(part * width + index * LANES, part * width + (index + 1) * LANES)
                    split[low:high, lanes] = wide[index, pl.ds(part, count, stride=2), :].astype(BF16)

    wait(0, qkv_n)
    query_product = mm(left[0:half, :], w_qkv[0])
    gram_and_tables()
    wait(qkv_n, 2 * qkv_n)
    key_product = mm(left[...], w_qkv[1, :, main])
    keep_turned(query_product, 0, 0, slice(0, width))
    wait(2 * qkv_n, 3 * qkv_n)
    value_product = mm(left[...], w_qkv[2, :, main])
    if shared < width:
        edge_product = mm(left[...], jnp.concatenate([w_qkv[1, :, edge], w_qkv[2, :, edge]], axis=1))
    keep_turned(key_product, 0, 1, main)
    keep_turned(key_product, half, 2, main)
    wait(3 * qkv_n, len(copies))
    if shared < width:
        keys, values = edge_product[:, : width - shared], edge_product[:, width - shared :]
        keep_turned(keys, 0, 1, edge)
        keep_turned(keys, half, 2, edge)
        keep(values, 0, 0, edge)
        keep(values, half, 1, edge)
    keep(value_product, 0, 0, main)
    keep(value_product, half, 1, main)
    divide(0, len(chunks))
    put(folds_out, folds_hbm)
    put(turned_out, turned_hbm)

    product = mm(states[...].reshape(2 * text, depth), split[...])
    for index in range(2 * lane_tiles):
        sums[index] = product[:, index * LANES : (index + 1) * LANES]
    gains = column_of(gains_ref, 2)
    padding = jnp.zeros((text_values_out.shape[1] - text, LANES), F32)
    for branch in range(2):
        for index in range(lane_tiles):
            lanes = slice(index * LANES, (index + 1) * LANES)
            rows = pl.ds(branch, text, stride=2)
            keys = jnp.concatenate([sums[index, rows, :], padding], axis=0).T
            text_keys_out[branch, lanes, :] = head_norm_down(keys, gains).astype(BF16)
            values = jnp.concatenate([sums[lane_tiles + index, rows, :], padding], axis=0)
            text_values_out[branch, :, lanes] = values.astype(BF16)
        put(text_keys_out.at[branch], text_keys_hbm.at[branch])
        put(text_values_out.at[branch], text_values_hbm.at[branch])
    for copy in out_copies:
        copy.wait()


def attend_kernel(
    live_ref,
    partner_ref,
    arrived_ref,
    place_ref,
    gram_ref,
    gains_ref,
    folds_hbm,
    turned_hbm,
    text_keys_hbm,
    text_values_hbm,
    keep_ref,
    send_ref,
    tokens_ref,
    folds_ref,
    turned_ref,
    text_keys_ref,
    text_values_ref,
    queries,
    keys,
    values,
    sems,
    *,
    text,
):
    copies = []
    for source, target in (
        (turned_hbm, turned_ref),
        (folds_hbm, folds_ref),
        (text_keys_hbm, text_keys_ref),
        (text_values_hbm, text_values_ref),
    ):
        copies.append(pltpu.make_async_copy(source, target, sems.at[len(copies)]))
        copies[-1].start()
    group, member = position()
    groups_n, _, block, narrow = arrived_ref.shape
    tiles = place_ref.shape[0] // 2
    rows = tiles * TILE
    half_rows = rows // 2
    width = keep_ref.shape[2]
    rest = text_values_ref.shape[1]
    mate = partner_ref[group]
    own_len = live_ref[group]
    mate_len = jnp.where(mate != group, live_ref[mate], 0)

    own_parts, mate_parts = [], []
    for turn in range(2):
        source = member ^ turn
        block_rows = arrived_ref[:, pl.ds(source, 1)].reshape(groups_n * block, narrow)
        found = mm(place_ref[...], block_rows)
        for parts, base in ((own_parts, 0), (mate_parts, tiles)):
            pair = found[base : base + tiles]
            parts.append(jnp.concatenate([pair[:, :CH], pair[:, :CH]], axis=1))
            parts.append(jnp.concatenate([pair[:, CH:], pair[:, CH:]], axis=1))
    own_tokens = jnp.concatenate(own_parts, axis=0)
    mate_tokens = jnp.concatenate(mate_parts, axis=0)
    tokens_ref[...] = own_tokens[:half_rows].astype(BF16)
    lane = iota((1, LANES), 1)

    def normed(tokens):
        narrow_tokens = tokens.astype(BF16)
        image = mm(narrow_tokens, gram_ref[0 : 2 * CH]) + mm(narrow_tokens, gram_ref[2 * CH :])
        variance = jnp.sum(image * tokens[:, :CH], axis=1, keepdims=True)
        scaled = tokens * lax.rsqrt(jnp.maximum(variance, 0.0) + EPS)
        high = scaled.astype(BF16).astype(F32)
        ones = jnp.where(lane < CH + 2, 1.0, 0.0)
        return jnp.concatenate([high, jnp.where(lane < CH, scaled - high, ones)], axis=1)

    own_normed = normed(own_tokens)
    mate_normed = normed(mate_tokens)
    own_turned = own_normed.T.astype(BF16)
    mate_turned = mate_normed.T.astype(BF16)
    own_normed = own_normed.astype(BF16)
    mate_normed = mate_normed.astype(BF16)

    row = iota((1, rows), 1)
    turn_of = row // half_rows
    inside = row - turn_of * half_rows
    second = inside // tiles
    slot = (inside - second * tiles) * TILE + 2 * (turn_of ^ member) + second
    own_dead = jnp.where(slot < own_len, 0.0, DEAD)
    mate_dead = jnp.where(slot < mate_len, 0.0, DEAD)
    text_dead = jnp.where(iota((1, rest), 1) < text, 0.0, DEAD)
    dead = jnp.concatenate([own_dead, mate_dead, text_dead], axis=1)
    dead = jnp.where(iota((PACK, 1), 0) == 0, dead, 0.0).astype(BF16)
    dead = jnp.concatenate([dead, jnp.zeros((HEAD - PACK, dead.shape[1]), BF16)], axis=0)

    even = lane < HEAD
    query_gains = column_of(gains_ref, 0) * (LOG2E * HEAD**-0.5)
    key_gains = column_of(gains_ref, 1)
    filling = jnp.zeros((CH - PACK, width), BF16)
    lane_tiles = width // LANES
    for copy in copies:
        copy.wait()

    def fold_of(branch, side):
        fold = folds_ref[branch, side]
        return jnp.concatenate([fold[: 2 * CH], fold[:CH], fold[2 * CH :], filling], axis=0)

    def project(branch):
        query = head_norm_down(mm(turned_ref[branch, 0], own_turned), query_gains)
        queries[branch] = query.T
        for side, turned in ((0, own_turned), (1, mate_turned)):
            key = head_norm_down(mm(turned_ref[branch, 1 + side], turned), key_gains)
            keys[branch, :, side * rows : (side + 1) * rows] = key.astype(BF16)
        keys[branch, :, 2 * rows :] = text_keys_ref[branch]
        values[branch, 0:rows, :] = mm(own_normed, fold_of(branch, 0)).astype(BF16)
        values[branch, rows : 2 * rows, :] = mm(mate_normed, fold_of(branch, 1)).astype(BF16)
        values[branch, 2 * rows :, :] = text_values_ref[branch]

    def score(branch, at, side):
        inside_head = even if side == 0 else jnp.logical_not(even)
        marker = lane == (HEAD if side == 0 else 0)
        query = queries[branch, :, at : at + LANES]
        query = jnp.where(inside_head, query, jnp.where(marker, 1.0, 0.0)).astype(BF16)
        first = at + side * HEAD
        one_keys = keys[branch, first : first + HEAD, :]
        return mm(query, jnp.concatenate([one_keys, dead] if side == 0 else [dead, one_keys], axis=0))

    outs = []

    def settle(branch, at, side, scores):
        inside_head = even if side == 0 else jnp.logical_not(even)
        one_values = values[branch, :, at : at + LANES]
        one_values = jnp.where(inside_head, one_values, jnp.ones_like(one_values))
        highest = jnp.max(scores, axis=1, keepdims=True)
        outs.append(mm(jnp.exp2(scores - highest).astype(BF16), one_values))
        if side == 1:
            first, second = outs
            outs.clear()
            total = jnp.where(even, second, first)
            total = jnp.concatenate([total[:, HEAD:], total[:, :HEAD]], axis=1)
            merged = (jnp.where(even, first, second) / total).astype(BF16)
            keep_ref[branch, :, at : at + LANES] = merged[:half_rows]
            send_ref[branch, :, at : at + LANES] = merged[half_rows:]

    waiting = None
    project(0)
    for branch in range(2):
        for pair in range(lane_tiles):
            for side in range(2):
                at = pair * LANES
                scores = score(branch, at, side)
                if waiting is not None:
                    settle(*waiting)
                waiting = (branch, at, side, scores)
            if branch == 0 and pair == lane_tiles // 2:
                project(1)
    settle(*waiting)


def finish_kernel(
    step,
    live_ref,
    kept_ref,
    came_ref,
    w_own_ref,
    w_came_ref,
    tokens_ref,
    embed_ref,
    mod_ref,
    w_final_ref,
    home_ref,
    out_ref,
    state,
):
    group, member = position()
    half_rows = tokens_ref.shape[0]
    tiles = home_ref.shape[0]
    width, depth = w_own_ref.shape
    both = 2 * half_rows
    chunks = spans(depth, step)
    kept = kept_ref[...].reshape(both, width)
    came = came_ref[...].reshape(both, width)

    def rows_of(index, low, high):
        first = jnp.broadcast_to(mod_ref[index, 0:1, low:high], (half_rows, high - low))
        second = jnp.broadcast_to(mod_ref[index, 1:2, low:high], (half_rows, high - low))
        return jnp.concatenate([first, second], axis=0)

    def folded(value):
        return sum(value[:, at : at + LANES] for at in range(0, value.shape[1], LANES))

    pivot = None
    total = jnp.zeros((both, LANES), F32)
    squares = jnp.zeros((both, LANES), F32)
    for turn, (low, high) in enumerate(chunks):
        mixed = mm(kept, w_own_ref[:, low:high]).astype(BF16).astype(F32) + mm(
            came, w_came_ref[:, low:high]
        ).astype(BF16).astype(F32)
        hidden = mm(tokens_ref[:, :CH], embed_ref[:, low:high])
        hidden = jnp.concatenate([hidden, hidden], axis=0)
        value = hidden + rows_of(2, low, high) * mixed
        if pivot is None:
            pivot = jnp.sum(folded(value), axis=1, keepdims=True) * (1.0 / (high - low))
        value = value - pivot
        state[:, low:high] = value
        total += folded(value)
        squares += folded(value * value)
    mean = jnp.sum(total, axis=1, keepdims=True) * (1.0 / depth)
    spread = jnp.sum(squares, axis=1, keepdims=True) * (1.0 / depth) - mean * mean
    scale = lax.rsqrt(jnp.maximum(spread, 0.0) + EPS)
    offset = -mean * scale
    velocity = jnp.zeros((both, CH), F32)
    for low, high in chunks:
        normed = state[:, low:high] * scale + offset
        final = normed * (1.0 + rows_of(4, low, high)) + rows_of(3, low, high)
        velocity += mm_nt(final.astype(BF16), w_final_ref[:, low:high])
    guided = velocity[half_rows:] + GUIDE * (velocity[:half_rows] - velocity[half_rows:])
    row = iota((half_rows, 1), 0)
    second = row // tiles
    slot = (row - second * tiles) * TILE + 2 * member + second
    guided = jnp.where(slot < live_ref[group], guided, 0.0)
    columns = jnp.concatenate([guided[:tiles], guided[tiles:]], axis=1).astype(BF16)
    out_ref[...] = mm_tn(home_ref[...], columns).astype(BF16)


def update_kernel(back, slots_ref, latents_ref, returned_ref, out_ref):
    tiles = latents_ref.shape[0]
    group, _ = position()
    target, rank = own_bucket(slots_ref, group, tiles)
    sender = one_hot(iota((returned_ref.shape[0], tiles), 0) == target * back + rank)
    out_ref[...] = latents_ref[...] + STEP * mm_tn(sender, returned_ref[...])


def shards(
    latents,
    tile_slot,
    live,
    partner,
    text_states,
    modulation,
    w_embed,
    w_qkv,
    w_text_kv,
    w_out,
    w_final,
    norm_gains,
):
    groups_n = lax.axis_size("groups")
    tiles, narrow = latents.shape
    rows = tiles * TILE
    depth = w_embed.shape[1]
    width = w_out.shape[0]
    text = text_states.shape[2]
    capacity = max(2, (tiles + groups_n - 1) // groups_n)
    block = round_up(2 * capacity, PACK)
    back = round_up(capacity, PACK)
    slots = tile_slot.reshape(groups_n * tiles // LANES, LANES)
    both = ("groups", "mp")
    cores = [(0, 1), (1, 0)]

    adaptive = jnp.swapaxes(modulation[0], 0, 1)
    pairs = [(source, source ^ 1) for source in range(groups_n)]
    mate_mod = lax.ppermute(adaptive, "groups", pairs)

    outbound = pl.pallas_call(
        functools.partial(send_kernel, capacity, block),
        out_shape=jax.ShapeDtypeStruct((groups_n, 2, block, narrow), BF16),
        in_specs=[spec(), spec()],
        out_specs=spec(),
        compiler_params=grant(SEND_MIB),
    )(slots, latents)
    arrived = lax.all_to_all(
        outbound.reshape(groups_n * 2, block, narrow), both, split_axis=0, concat_axis=0, tiled=True
    ).reshape(groups_n, 2, block, narrow)

    step = 4 * LANES
    chunk_n = len(spans(depth, step))
    qkv_n = len(spans(depth, 2 * step))
    left_rows = 2 * (2 * CH + PACK)
    rest = round_up(2 * rows + text, 2 * LANES) - 2 * rows
    kept_shapes = [
        jax.ShapeDtypeStruct((2, 2, 2 * CH + PACK, width), BF16),
        jax.ShapeDtypeStruct((2, 3, width, 4 * CH), BF16),
        jax.ShapeDtypeStruct((2, width, rest), BF16),
        jax.ShapeDtypeStruct((2, rest, width), BF16),
    ]
    gram, place, home, folds, turned, text_keys, text_values = pl.pallas_call(
        functools.partial(prepare_kernel, capacity, block, back, step),
        out_shape=[
            jax.ShapeDtypeStruct((4 * CH, CH), BF16),
            jax.ShapeDtypeStruct((2 * tiles, groups_n * block), BF16),
            jax.ShapeDtypeStruct((tiles, groups_n * back), BF16),
            *kept_shapes,
        ],
        in_specs=[spec()] * 5 + [spec(pltpu.HBM)] * 3,
        out_specs=[spec()] * 3 + [spec(pltpu.HBM)] * 4,
        scratch_shapes=[
            *(pltpu.VMEM(kept.shape, BF16) for kept in kept_shapes),
            pltpu.VMEM((text, 2, depth), BF16),
            pltpu.VMEM((2 * depth, width), BF16),
            pltpu.VMEM((3, depth, width), BF16),
            pltpu.VMEM((width // LANES, 2 * step, LANES), F32),
            pltpu.VMEM((depth, 2 * width), BF16),
            pltpu.VMEM((2 * width // LANES, 2 * text, LANES), F32),
            pltpu.VMEM((left_rows, depth), BF16),
            pltpu.SemaphoreType.DMA((1 + chunk_n + 3 * qkv_n,)),
            pltpu.SemaphoreType.DMA((6,)),
        ],
        compiler_params=grant(PREPARE_MIB),
        cost_estimate=pl.CostEstimate(
            flops=2 * (left_rows * 3 + 4 * text) * depth * width,
            bytes_accessed=2 * depth * 5 * width,
            transcendentals=0,
        ),
    )(
        slots,
        w_embed,
        adaptive,
        mate_mod,
        norm_gains,
        jnp.swapaxes(text_states[0], 0, 1),
        w_text_kv,
        jnp.swapaxes(w_qkv, 0, 1),
    )

    arrived, gram, w_out_sent = lax.optimization_barrier((arrived, gram, w_out))
    came_w_out = lax.ppermute(w_out_sent, "mp", cores)
    half = jax.ShapeDtypeStruct((2, rows // 2, width), BF16)
    kept, sent, tokens = pl.pallas_call(
        functools.partial(attend_kernel, text=text),
        out_shape=[half, half, jax.ShapeDtypeStruct((rows // 2, 2 * CH), BF16)],
        in_specs=[spec(pltpu.SMEM)] * 2 + [spec()] * 4 + [spec(pltpu.HBM)] * 4,
        out_specs=[spec()] * 3,
        scratch_shapes=[
            pltpu.VMEM(folds.shape, BF16),
            pltpu.VMEM(turned.shape, BF16),
            pltpu.VMEM(text_keys.shape, BF16),
            pltpu.VMEM(text_values.shape, BF16),
            pltpu.VMEM((2, rows, width), F32),
            pltpu.VMEM((2, width, 2 * rows + rest), BF16),
            pltpu.VMEM((2, 2 * rows + rest, width), BF16),
            pltpu.SemaphoreType.DMA((4,)),
        ],
        compiler_params=grant(ATTEND_MIB),
        cost_estimate=pl.CostEstimate(
            flops=40 * 2 * 2 * rows * (2 * rows + rest) * width,
            bytes_accessed=8 * MIB,
            transcendentals=0,
        ),
    )(live, partner, arrived, place, gram, norm_gains, folds, turned, text_keys, text_values)
    came = lax.ppermute(sent, "mp", cores)

    homeward = pl.pallas_call(
        functools.partial(finish_kernel, step),
        out_shape=jax.ShapeDtypeStruct((groups_n * back, narrow), BF16),
        in_specs=[spec(pltpu.SMEM)] + [spec()] * 9,
        out_specs=spec(),
        scratch_shapes=[
            pltpu.VMEM((rows, depth), F32),
        ],
        compiler_params=grant(FINISH_MIB),
    )(live, kept, came, w_out, came_w_out, tokens, w_embed, adaptive, w_final.T, home)
    returned = lax.all_to_all(
        homeward.reshape(groups_n, back, narrow), "groups", split_axis=0, concat_axis=0, tiled=True
    ).reshape(groups_n * back, narrow)
    return pl.pallas_call(
        functools.partial(update_kernel, back),
        out_shape=jax.ShapeDtypeStruct((tiles, narrow), F32),
        in_specs=[spec()] * 3,
        out_specs=spec(),
        compiler_params=grant(UPDATE_MIB),
    )(slots, latents, returned)


def solution(mesh):
    placed = (
        P("groups", "mp"),
        P(),
        P(),
        P(),
        P("groups", None, None, None),
        P("groups", None, None, None),
        P(),
        P(None, None, "mp"),
        P(None, None, "mp"),
        P("mp", None),
        P(),
        P(),
    )
    return jax.shard_map(
        shards, mesh=mesh, in_specs=placed, out_specs=P("groups", "mp"), check_vma=False
    )
```

```python
import functools
import math

import jax
import jax.numpy as jnp
from jax import lax
from jax.experimental import pallas as pl
from jax.experimental.pallas import tpu as pltpu
from jax.sharding import PartitionSpec as P

HEAD = 64
CH = 64
TILE = 4
LANES = 128
PACK = 16

GUIDE = 3.5
STEP = -0.25
EPS = 1e-06
LOG2E = 1.4426950408889634
DEAD = -1e30
SEND_MIB, PREPARE_MIB, ATTEND_MIB, FINISH_MIB, UPDATE_MIB = 60, 56, 52, 24, 16

F32 = jnp.float32
BF16 = jnp.bfloat16
MIB = 2**20


def round_up(value, step):
    return (value + step - 1) // step * step


def spans(total, step):
    return [(start, min(start + step, total)) for start in range(0, total, step)]


def mm(left, right):
    return jnp.dot(left, right, preferred_element_type=F32)


def mm_nt(left, right):
    return lax.dot_general(left, right, (((1,), (1,)), ((), ())), preferred_element_type=F32)


def mm_tn(left, right):
    return lax.dot_general(left, right, (((0,), (0,)), ((), ())), preferred_element_type=F32)


def iota(shape, dim):
    return lax.broadcasted_iota(jnp.int32, shape, dim)


def two_terms(value):
    high = value.astype(BF16)
    return high, (value - high.astype(F32)).astype(BF16)


def one_hot(mask):
    return jnp.where(mask, 1.0, 0.0).astype(BF16)


def spec(space=pltpu.VMEM):
    return pl.BlockSpec(memory_space=space)


def grant(mib):
    return pltpu.CompilerParams(vmem_limit_bytes=mib * MIB)


def position():
    return lax.axis_index("groups").astype(jnp.int32), lax.axis_index("mp").astype(jnp.int32)


def head_norm(value, gains):
    wide = value.shape[1]
    same = iota((wide, wide), 0) // HEAD == iota((wide, wide), 1) // HEAD
    averaging = jnp.where(same, 1.0 / HEAD, 0.0).astype(BF16)
    square = mm((value * value).astype(BF16), averaging)
    return value * (lax.rsqrt(square + EPS) * gains)


def lanes_of(gains, wide):
    return jnp.concatenate([gains] * (wide // HEAD), axis=1)


def column_of(gains_ref, index):
    row = jnp.broadcast_to(gains_ref[index : index + 1, :], (LANES, HEAD))
    return row.T[:, 0:1]


def head_norm_down(value, gains):
    parts = []
    for at in range(0, value.shape[0], HEAD):
        head = value[at : at + HEAD]
        square = jnp.sum(head * head, axis=0, keepdims=True) * (1.0 / HEAD)
        parts.append(head * lax.rsqrt(square + EPS) * gains)
    return jnp.concatenate(parts, axis=0)


def own_bucket(slots_ref, group, tiles):
    first = group * tiles
    row = first // LANES
    after = jnp.minimum(row + 1, slots_ref.shape[0] - 1)
    window = jnp.concatenate([slots_ref[pl.ds(row, 1), :], slots_ref[pl.ds(after, 1), :]], axis=1)
    turn = 2 * LANES - (first - row * LANES)
    slots = pltpu.roll(window, turn, 1)[:, :tiles]
    target = slots // tiles
    across = target.astype(F32)
    diagonal = iota((tiles, tiles), 0) == iota((tiles, tiles), 1)
    down = jnp.sum(jnp.where(diagonal, across, 0.0), axis=1, keepdims=True)
    earlier = (down == across) & (iota((tiles, tiles), 0) < iota((tiles, tiles), 1))
    rank = jnp.sum(jnp.where(earlier, 1.0, 0.0), axis=0, keepdims=True).astype(jnp.int32)
    return target, rank


def send_kernel(capacity, block, slots_ref, latents_ref, out_ref):
    tiles = latents_ref.shape[0]
    groups_n = out_ref.shape[0]
    group, _ = position()
    target, rank = own_bucket(slots_ref, group, tiles)
    rows = groups_n * block
    bucket = iota((rows, tiles), 0)
    first = target * block + rank
    second = (target ^ 1) * block + capacity + rank
    sender = one_hot((bucket == first) | (bucket == second))
    sent = mm(sender, latents_ref[...].astype(BF16)).astype(BF16).reshape(groups_n, block, -1)
    out_ref[:, 0] = sent
    out_ref[:, 1] = sent


def slots_by_group(slots_ref, tiles):
    per = LANES // math.gcd(tiles, LANES)
    rows_per = per * tiles // LANES
    repeats = slots_ref.shape[0] // rows_per
    wide = jnp.concatenate(
        [slots_ref[pl.ds(row, repeats, stride=rows_per), :] for row in range(rows_per)], axis=1
    )
    parts = [wide[:, turn * tiles : (turn + 1) * tiles] for turn in range(per)]
    return jnp.concatenate(parts, axis=0), lambda row: per * (row % repeats) + row // repeats


def tables(slots, group_of, group, capacity, block, offset):
    groups_n, tiles = slots.shape
    target = slots // tiles
    placed = slots - target * tiles
    mine = target == group
    before = one_hot(iota((tiles, tiles), 0) < iota((tiles, tiles), 1))
    rank = jnp.where(mine, mm(one_hot(mine), before), float(capacity))
    columns = groups_n * block
    spread = one_hot(iota((groups_n, columns), 1) // block == group_of(iota((groups_n, columns), 0)))
    rank_of = mm_tn(rank.astype(BF16), spread)
    place_of = mm_tn(placed.astype(F32).astype(BF16), spread)
    level = (iota((tiles, columns), 1) % block - offset).astype(F32)
    hit = (rank_of == level) & (level >= 0.0) & (level < capacity)
    place = jnp.sum(jnp.where(hit, place_of + 1.0, 0.0), axis=0, keepdims=True) - 1.0
    return one_hot(iota((tiles, columns), 0).astype(F32) == place)


def prepare_kernel(
    capacity,
    block,
    back,
    step,
    slots_hbm,
    embed_hbm,
    own_mod_hbm,
    mate_mod_hbm,
    gains_hbm,
    states_hbm,
    w_text_hbm,
    w_qkv_hbm,
    home_out,
    rows_hbm,
    turned_hbm,
    slots_ref,
    embed_ref,
    own_mod_ref,
    mate_mod_ref,
    gains_ref,
    rows_out,
    turned_out,
    states,
    mingled,
    w_qkv,
    wide,
    split,
    sums,
    left,
    sems,
    out_sems,
    small_sems,
):
    depth = embed_ref.shape[1]
    width = w_qkv.shape[2]
    text = states.shape[0]
    tiles = home_out.shape[0]
    group, _ = position()
    own_rows = 2 * CH
    half = own_rows + PACK
    fold_rows = 2 * CH + PACK
    chunks = spans(depth, step)
    lane_tiles = width // LANES

    small = (
        (embed_hbm, embed_ref),
        (own_mod_hbm, own_mod_ref),
        (mate_mod_hbm, mate_mod_ref),
        (slots_hbm, slots_ref),
        (gains_hbm, gains_ref),
    )
    small = [
        pltpu.make_async_copy(source, target, small_sems.at[index])
        for index, (source, target) in enumerate(small)
    ]
    for copy in small:
        copy.start()
    sources = []

    def qkv_source(part):
        for low, high in spans(depth, 2 * step):
            rows = pl.ds(low, high - low)
            sources.append((w_qkv_hbm.at[part, rows], w_qkv.at[part, rows]))
        return len(sources)

    query_end = qkv_source(0)
    sources.append((states_hbm, states))
    w_mingled = w_text_hbm.reshape(2 * depth, width)
    for low, high in chunks:
        rows = pl.ds(2 * low, 2 * (high - low))
        sources.append((w_mingled.at[rows], mingled.at[rows]))
    text_end = len(sources)
    qkv_source(1)
    value_end = qkv_source(2)
    copies = [
        pltpu.make_async_copy(source, target, sems.at[index])
        for index, (source, target) in enumerate(sources)
    ]
    for copy in copies:
        copy.start()

    def wait(first, last):
        for index in range(first, last):
            copies[index].wait()

    for copy in small:
        copy.wait()

    embed = embed_ref[...].astype(F32)
    centred = embed - jnp.mean(embed, axis=1, keepdims=True)
    for side, mod_ref in ((0, own_mod_ref), (1, mate_mod_ref)):
        base = side * half
        for branch in range(2):
            scaled = centred * (1.0 + mod_ref[1, branch : branch + 1, :])
            left[pl.ds(base + branch * CH, CH), :] = scaled.astype(BF16)
        high, low = two_terms(mod_ref[0])
        shifts = jnp.concatenate([high.astype(F32), low.astype(F32)], axis=0)
        shifts = jnp.concatenate([shifts, jnp.zeros((PACK - 4, depth), F32)], axis=0)
        left[pl.ds(base + own_rows, PACK), :] = shifts.astype(BF16)
    def pieces(product, base, branch):
        first = base + own_rows + branch
        bias = two_terms(product[first : first + 1] + product[first + 2 : first + 3])
        fold = two_terms(product[base + branch * CH : base + (branch + 1) * CH])
        return [part.astype(F32) for part in fold + bias]

    def keep(product, base, side, lanes):
        for branch in range(2):
            zeros = jnp.zeros((PACK - 2, product.shape[1]), F32)
            stacked = jnp.concatenate(pieces(product, base, branch) + [zeros], axis=0)
            at = side * fold_rows
            rows_out[branch, at : at + fold_rows, lanes] = stacked.astype(BF16)

    def keep_turned(product, base, kind, lanes):
        for branch in range(2):
            high, low, bias_high, bias_low = pieces(product, base, branch)
            zeros = jnp.zeros((CH - 2, product.shape[1]), F32)
            stacked = jnp.concatenate([high, low, high, bias_high, bias_low, zeros], axis=0)
            turned_out[branch, kind, lanes, :] = stacked.T.astype(BF16)

    shared = width // (2 * LANES) * (2 * LANES)
    main, edge = slice(0, shared), slice(shared, width)
    def gram_and_tables():
        high, low = two_terms(centred)
        parts = (mm_nt(high, high) + (mm_nt(high, low) + mm_nt(low, high))) * (1.0 / depth)
        top, rest = two_terms(parts)
        bottom = (parts - top.astype(F32) - rest.astype(F32)).astype(BF16)
        gram = jnp.concatenate([top, rest, bottom, jnp.zeros((CH, CH), BF16)], axis=1)
        turned_out[0, 4, 2 * tiles : 2 * tiles + CH, :] = gram
        slots, group_of = slots_by_group(slots_ref, tiles)
        lanes_n = turned_out.shape[3]
        for side in range(2):
            place = tables(slots, group_of, group ^ side, capacity, block, side * capacity)
            for turn, (low, high) in enumerate(spans(place.shape[1], lanes_n)):
                turned_out[0, 4 + turn, side * tiles : (side + 1) * tiles, 0 : high - low] = place[:, low:high]
        home_out[...] = tables(slots, group_of, group, capacity, back, 0)

    out_copies = []

    def put(source, target):
        out_copies.append(pltpu.make_async_copy(source, target, out_sems.at[len(out_copies)]))
        out_copies[-1].start()

    def divide():
        for turn, (low, high) in enumerate(chunks):
            at = query_end + 1 + turn
            wait(at, at + 1)
            count = high - low
            for index in range(lane_tiles):
                lanes = slice(index * LANES, (index + 1) * LANES)
                wide[index, 0 : 2 * count, :] = mingled[2 * low : 2 * high, lanes].astype(F32)
            for part in range(2):
                for index in range(lane_tiles):
                    lanes = slice(part * width + index * LANES, part * width + (index + 1) * LANES)
                    split[low:high, lanes] = wide[index, pl.ds(part, count, stride=2), :].astype(BF16)

    gram_and_tables()
    wait(0, query_end + 1)
    query_product = mm(left[0:half, :], w_qkv[0])
    divide()
    keep_turned(query_product, 0, 0, slice(0, width))

    product = mm(states[...].reshape(2 * text, depth), split[...])
    for index in range(2 * lane_tiles):
        sums[index] = product[:, index * LANES : (index + 1) * LANES]
    wait(text_end, value_end)
    key_product = mm(left[...], w_qkv[1, :, main])
    gains = column_of(gains_ref, 2)
    padding = jnp.zeros((turned_out.shape[3] - text, LANES), F32)
    for branch in range(2):
        for index in range(lane_tiles):
            lanes = slice(index * LANES, (index + 1) * LANES)
            rows = pl.ds(branch, text, stride=2)
            keys = jnp.concatenate([sums[index, rows, :], padding], axis=0).T
            turned_out[branch, 3, lanes, :] = head_norm_down(keys, gains).astype(BF16)
            values = jnp.concatenate([sums[lane_tiles + index, rows, :], padding], axis=0)
            rows_out[branch, 2 * fold_rows :, lanes] = values.astype(BF16)
    keep_turned(key_product, 0, 1, main)
    keep_turned(key_product, half, 2, main)
    value_product = mm(left[...], w_qkv[2, :, main])
    put(turned_out.at[0, pl.ds(4, turned_out.shape[1] - 4)], turned_hbm.at[0, pl.ds(4, turned_out.shape[1] - 4)])
    if shared < width:
        edge_product = mm(left[...], jnp.concatenate([w_qkv[1, :, edge], w_qkv[2, :, edge]], axis=1))
    keep(value_product, 0, 0, main)
    keep(value_product, half, 1, main)
    if shared < width:
        keys, values = edge_product[:, : width - shared], edge_product[:, width - shared :]
        keep_turned(keys, 0, 1, edge)
        keep_turned(keys, half, 2, edge)
        keep(values, 0, 0, edge)
        keep(values, half, 1, edge)
    for branch in range(2):
        put(turned_out.at[branch, pl.ds(0, 4)], turned_hbm.at[branch, pl.ds(0, 4)])
        put(rows_out.at[branch], rows_hbm.at[branch])
    for copy in out_copies:
        copy.wait()


def attend_kernel(
    live_ref,
    partner_ref,
    arrived_ref,
    gains_ref,
    rows_hbm,
    turned_hbm,
    keep_ref,
    send_ref,
    tokens_ref,
    rows_ref,
    turned_ref,
    queries,
    keys,
    values,
    sems,
    *,
    text,
):
    def fetch(source, target, index):
        copy = pltpu.make_async_copy(source, target, sems.at[index])
        copy.start()
        return copy

    tables_n = turned_hbm.shape[1] - 4
    tables_at = (0, pl.ds(4, tables_n))
    tables_copy = fetch(turned_hbm.at[tables_at], turned_ref.at[tables_at], 0)
    copies = [
        (
            fetch(turned_hbm.at[branch, pl.ds(0, 4)], turned_ref.at[branch, pl.ds(0, 4)], 1 + 2 * branch),
            fetch(rows_hbm.at[branch], rows_ref.at[branch], 2 + 2 * branch),
        )
        for branch in range(2)
    ]
    group, member = position()
    groups_n, _, block, narrow = arrived_ref.shape
    rest = turned_ref.shape[3]
    half_rows = tokens_ref.shape[0]
    rows = 2 * half_rows
    tiles = rows // TILE
    width = keep_ref.shape[2]
    fold_rows = 2 * CH + PACK
    mate = partner_ref[group]
    own_len = live_ref[group]
    mate_len = jnp.where(mate != group, live_ref[mate], 0)

    own_parts, mate_parts = [], []
    tables_copy.wait()
    gram = turned_ref[0, 4, 2 * tiles : 2 * tiles + CH, :]
    for turn in range(2):
        source = member ^ turn
        block_rows = arrived_ref[:, pl.ds(source, 1)].reshape(groups_n * block, narrow)
        found = sum(
            mm(turned_ref[0, 4 + turn, 0 : 2 * tiles, 0 : high - low], block_rows[low:high])
            for turn, (low, high) in enumerate(spans(groups_n * block, rest))
        )
        for parts, base in ((own_parts, 0), (mate_parts, tiles)):
            pair = found[base : base + tiles]
            parts.append(jnp.concatenate([pair[:, :CH], pair[:, :CH]], axis=1))
            parts.append(jnp.concatenate([pair[:, CH:], pair[:, CH:]], axis=1))
    own_tokens = jnp.concatenate(own_parts, axis=0)
    mate_tokens = jnp.concatenate(mate_parts, axis=0)
    tokens_ref[...] = own_tokens[:half_rows].astype(BF16)
    lane = iota((1, LANES), 1)

    def normed(tokens):
        image = mm(tokens[:, :CH].astype(BF16), gram)
        image = (image[:, :LANES] + image[:, LANES:]) * tokens
        variance = jnp.sum(image, axis=1, keepdims=True)
        scaled = tokens * lax.rsqrt(jnp.maximum(variance, 0.0) + EPS)
        high = scaled.astype(BF16).astype(F32)
        ones = jnp.where(lane < CH + 2, 1.0, 0.0)
        return jnp.concatenate([high, jnp.where(lane < CH, scaled - high, ones)], axis=1)

    own_normed = normed(own_tokens)
    mate_normed = normed(mate_tokens)
    own_turned = own_normed.T.astype(BF16)
    mate_turned = mate_normed.T.astype(BF16)
    own_normed = own_normed.astype(BF16)
    mate_normed = mate_normed.astype(BF16)

    row = iota((1, rows), 1)
    turn_of = row // half_rows
    inside = row - turn_of * half_rows
    second = inside // tiles
    slot = (inside - second * tiles) * TILE + 2 * (turn_of ^ member) + second
    own_dead = jnp.where(slot < own_len, 0.0, DEAD)
    mate_dead = jnp.where(slot < mate_len, 0.0, DEAD)
    text_dead = jnp.where(iota((1, rest), 1) < text, 0.0, DEAD)
    dead = jnp.concatenate([own_dead, mate_dead, text_dead], axis=1)
    dead = jnp.where(iota((PACK, 1), 0) == 0, dead, 0.0).astype(BF16)
    dead = jnp.concatenate([dead, jnp.zeros((HEAD - PACK, dead.shape[1]), BF16)], axis=0)

    even = lane < HEAD
    query_gains = column_of(gains_ref, 0) * (LOG2E * HEAD**-0.5)
    key_gains = column_of(gains_ref, 1)
    filling = jnp.zeros((CH - PACK, width), BF16)
    lane_tiles = width // LANES

    def fold_of(branch, side):
        fold = rows_ref[branch, side * fold_rows : (side + 1) * fold_rows, :]
        return jnp.concatenate([fold[: 2 * CH], fold[:CH], fold[2 * CH :], filling], axis=0)

    def project(branch):
        for copy in copies[branch]:
            copy.wait()
        query = head_norm_down(mm(turned_ref[branch, 0], own_turned), query_gains)
        queries[branch] = query.T
        for side, turned in ((0, own_turned), (1, mate_turned)):
            key = head_norm_down(mm(turned_ref[branch, 1 + side], turned), key_gains)
            keys[branch, :, side * rows : (side + 1) * rows] = key.astype(BF16)
        keys[branch, :, 2 * rows :] = turned_ref[branch, 3]
        values[branch, 0:rows, :] = mm(own_normed, fold_of(branch, 0)).astype(BF16)
        values[branch, rows : 2 * rows, :] = mm(mate_normed, fold_of(branch, 1)).astype(BF16)
        values[branch, 2 * rows :, :] = rows_ref[branch, 2 * fold_rows :, :]

    def score(branch, at, side):
        inside_head = even if side == 0 else jnp.logical_not(even)
        marker = lane == (HEAD if side == 0 else 0)
        query = queries[branch, :, at : at + LANES]
        query = jnp.where(inside_head, query, jnp.where(marker, 1.0, 0.0)).astype(BF16)
        first = at + side * HEAD
        one_keys = keys[branch, first : first + HEAD, :]
        return mm(query, jnp.concatenate([one_keys, dead] if side == 0 else [dead, one_keys], axis=0))

    outs = []

    def settle(branch, at, side, scores):
        inside_head = even if side == 0 else jnp.logical_not(even)
        one_values = values[branch, :, at : at + LANES]
        one_values = jnp.where(inside_head, one_values, jnp.ones_like(one_values))
        highest = jnp.max(scores, axis=1, keepdims=True)
        outs.append(mm(jnp.exp2(scores - highest).astype(BF16), one_values))
        if side == 1:
            first, second = outs
            outs.clear()
            total = jnp.where(even, second, first)
            total = jnp.concatenate([total[:, HEAD:], total[:, :HEAD]], axis=1)
            merged = (jnp.where(even, first, second) / total).astype(BF16)
            keep_ref[branch, :, at : at + LANES] = merged[:half_rows]
            send_ref[branch, :, at : at + LANES] = merged[half_rows:]

    waiting = None
    project(0)
    for branch in range(2):
        for pair in range(lane_tiles):
            for side in range(2):
                at = pair * LANES
                scores = score(branch, at, side)
                if waiting is not None:
                    settle(*waiting)
                waiting = (branch, at, side, scores)
            if branch == 0 and pair == lane_tiles // 2:
                project(1)
    settle(*waiting)


def finish_kernel(
    step,
    live_ref,
    kept_ref,
    came_ref,
    w_own_ref,
    w_came_ref,
    tokens_ref,
    embed_ref,
    mod_ref,
    w_final_ref,
    home_ref,
    out_ref,
    state,
):
    group, member = position()
    half_rows = tokens_ref.shape[0]
    tiles = home_ref.shape[0]
    width, depth = w_own_ref.shape
    both = 2 * half_rows
    chunks = spans(depth, step)
    attended = jnp.concatenate(
        [kept_ref[...].reshape(both, width), came_ref[...].reshape(both, width)], axis=1
    )

    def rows_of(index, low, high):
        first = jnp.broadcast_to(mod_ref[index, 0:1, low:high], (half_rows, high - low))
        second = jnp.broadcast_to(mod_ref[index, 1:2, low:high], (half_rows, high - low))
        return jnp.concatenate([first, second], axis=0)

    def folded(value):
        return sum(value[:, at : at + LANES] for at in range(0, value.shape[1], LANES))

    pivot = None
    total = jnp.zeros((both, LANES), F32)
    squares = jnp.zeros((both, LANES), F32)
    for low, high in chunks:
        weights = jnp.concatenate([w_own_ref[:, low:high], w_came_ref[:, low:high]], axis=0)
        mixed = mm(attended, weights)
        hidden = mm(tokens_ref[:, :CH], embed_ref[:, low:high])
        hidden = jnp.concatenate([hidden, hidden], axis=0)
        value = hidden + rows_of(2, low, high) * mixed
        if pivot is None:
            pivot = jnp.sum(folded(value), axis=1, keepdims=True) * (1.0 / (high - low))
        value = value - pivot
        state[:, low:high] = value
        total += folded(value)
        squares += folded(value * value)
    mean = jnp.sum(total, axis=1, keepdims=True) * (1.0 / depth)
    spread = jnp.sum(squares, axis=1, keepdims=True) * (1.0 / depth) - mean * mean
    scale = lax.rsqrt(jnp.maximum(spread, 0.0) + EPS)
    offset = -mean * scale
    velocity = jnp.zeros((both, CH), F32)
    for low, high in chunks:
        normed = state[:, low:high] * scale + offset
        final = normed * (1.0 + rows_of(4, low, high)) + rows_of(3, low, high)
        velocity += mm_nt(final.astype(BF16), w_final_ref[:, low:high])
    guided = velocity[half_rows:] + GUIDE * (velocity[:half_rows] - velocity[half_rows:])
    row = iota((half_rows, 1), 0)
    second = row // tiles
    slot = (row - second * tiles) * TILE + 2 * member + second
    guided = jnp.where(slot < live_ref[group], guided, 0.0)
    columns = jnp.concatenate([guided[:tiles], guided[tiles:]], axis=1).astype(BF16)
    out_ref[...] = mm_tn(home_ref[...], columns).astype(BF16)


def update_kernel(back, slots_ref, latents_ref, returned_ref, out_ref):
    tiles = latents_ref.shape[0]
    group, _ = position()
    target, rank = own_bucket(slots_ref, group, tiles)
    sender = one_hot(iota((returned_ref.shape[0], tiles), 0) == target * back + rank)
    out_ref[...] = latents_ref[...] + STEP * mm_tn(sender, returned_ref[...])


def shards(
    latents,
    tile_slot,
    live,
    partner,
    text_states,
    modulation,
    w_embed,
    w_qkv,
    w_text_kv,
    w_out,
    w_final,
    norm_gains,
):
    groups_n = lax.axis_size("groups")
    tiles, narrow = latents.shape
    rows = tiles * TILE
    depth = w_embed.shape[1]
    width = w_out.shape[0]
    text = text_states.shape[2]
    capacity = max(2, (tiles + groups_n - 1) // groups_n)
    block = round_up(2 * capacity, PACK)
    back = round_up(capacity, PACK)
    slots = tile_slot.reshape(groups_n * tiles // LANES, LANES)
    both = ("groups", "mp")
    cores = [(0, 1), (1, 0)]

    adaptive = jnp.swapaxes(modulation[0], 0, 1)
    pairs = [(source, source ^ 1) for source in range(groups_n)]
    mate_mod = lax.ppermute(adaptive, "groups", pairs)

    outbound = pl.pallas_call(
        functools.partial(send_kernel, capacity, block),
        out_shape=jax.ShapeDtypeStruct((groups_n, 2, block, narrow), BF16),
        in_specs=[spec(), spec()],
        out_specs=spec(),
        compiler_params=grant(SEND_MIB),
    )(slots, latents)
    arrived = lax.all_to_all(
        outbound.reshape(groups_n * 2, block, narrow), both, split_axis=0, concat_axis=0, tiled=True
    ).reshape(groups_n, 2, block, narrow)

    step = 4 * LANES
    chunk_n = len(spans(depth, step))
    qkv_n = len(spans(depth, 2 * step))
    left_rows = 2 * (2 * CH + PACK)
    rest = round_up(2 * rows + text, 2 * LANES) - 2 * rows
    rows_shape = (2, 2 * (2 * CH + PACK) + rest, width)
    turned_shape = (2, 4 + len(spans(groups_n * block, rest)), width, rest)
    home, rows_kit, turned_kit = pl.pallas_call(
        functools.partial(prepare_kernel, capacity, block, back, step),
        out_shape=[
            jax.ShapeDtypeStruct((tiles, groups_n * back), BF16),
            jax.ShapeDtypeStruct(rows_shape, BF16),
            jax.ShapeDtypeStruct(turned_shape, BF16),
        ],
        in_specs=[spec(pltpu.HBM)] * 8,
        out_specs=[spec()] + [spec(pltpu.HBM)] * 2,
        scratch_shapes=[
            pltpu.VMEM(slots.shape, jnp.int32),
            pltpu.VMEM(w_embed.shape, BF16),
            pltpu.VMEM(adaptive.shape, F32),
            pltpu.VMEM(adaptive.shape, F32),
            pltpu.VMEM(norm_gains.shape, F32),
            pltpu.VMEM(rows_shape, BF16),
            pltpu.VMEM(turned_shape, BF16),
            pltpu.VMEM((text, 2, depth), BF16),
            pltpu.VMEM((2 * depth, width), BF16),
            pltpu.VMEM((3, depth, width), BF16),
            pltpu.VMEM((width // LANES, 2 * step, LANES), F32),
            pltpu.VMEM((depth, 2 * width), BF16),
            pltpu.VMEM((2 * width // LANES, 2 * text, LANES), F32),
            pltpu.VMEM((left_rows, depth), BF16),
            pltpu.SemaphoreType.DMA((1 + chunk_n + 3 * qkv_n,)),
            pltpu.SemaphoreType.DMA((7,)),
            pltpu.SemaphoreType.DMA((5,)),
        ],
        compiler_params=grant(PREPARE_MIB),
        cost_estimate=pl.CostEstimate(
            flops=2 * (left_rows * 3 + 4 * text) * depth * width,
            bytes_accessed=2 * depth * 5 * width,
            transcendentals=0,
        ),
    )(
        slots,
        w_embed,
        adaptive,
        mate_mod,
        norm_gains,
        jnp.swapaxes(text_states[0], 0, 1),
        w_text_kv,
        jnp.swapaxes(w_qkv, 0, 1),
    )

    arrived, rows_kit, w_out_sent = lax.optimization_barrier((arrived, rows_kit, w_out))
    came_w_out = lax.ppermute(w_out_sent, "mp", cores)
    half = jax.ShapeDtypeStruct((2, rows // 2, width), BF16)
    kept, sent, tokens = pl.pallas_call(
        functools.partial(attend_kernel, text=text),
        out_shape=[half, half, jax.ShapeDtypeStruct((rows // 2, 2 * CH), BF16)],
        in_specs=[spec(pltpu.SMEM)] * 2 + [spec()] * 2 + [spec(pltpu.HBM)] * 2,
        out_specs=[spec()] * 3,
        scratch_shapes=[
            pltpu.VMEM(rows_shape, BF16),
            pltpu.VMEM(turned_shape, BF16),
            pltpu.VMEM((2, rows, width), F32),
            pltpu.VMEM((2, width, 2 * rows + rest), BF16),
            pltpu.VMEM((2, 2 * rows + rest, width), BF16),
            pltpu.SemaphoreType.DMA((5,)),
        ],
        compiler_params=grant(ATTEND_MIB),
        cost_estimate=pl.CostEstimate(
            flops=40 * 2 * 2 * rows * (2 * rows + rest) * width,
            bytes_accessed=8 * MIB,
            transcendentals=0,
        ),
    )(live, partner, arrived, norm_gains, rows_kit, turned_kit)
    came = lax.ppermute(sent, "mp", cores)

    homeward = pl.pallas_call(
        functools.partial(finish_kernel, step),
        out_shape=jax.ShapeDtypeStruct((groups_n * back, narrow), BF16),
        in_specs=[spec(pltpu.SMEM)] + [spec()] * 9,
        out_specs=spec(),
        scratch_shapes=[
            pltpu.VMEM((rows, depth), F32),
        ],
        compiler_params=grant(FINISH_MIB),
    )(live, kept, came, w_out, came_w_out, tokens, w_embed, adaptive, w_final.T, home)
    returned = lax.all_to_all(
        homeward.reshape(groups_n, back, narrow), "groups", split_axis=0, concat_axis=0, tiled=True
    ).reshape(groups_n * back, narrow)
    return pl.pallas_call(
        functools.partial(update_kernel, back),
        out_shape=jax.ShapeDtypeStruct((tiles, narrow), F32),
        in_specs=[spec()] * 3,
        out_specs=spec(),
        compiler_params=grant(UPDATE_MIB),
    )(slots, latents, returned)


def solution(mesh):
    placed = (
        P("groups", "mp"),
        P(),
        P(),
        P(),
        P("groups", None, None, None),
        P("groups", None, None, None),
        P(),
        P(None, None, "mp"),
        P(None, None, "mp"),
        P("mp", None),
        P(),
        P(),
    )
    return jax.shard_map(
        shards, mesh=mesh, in_specs=placed, out_specs=P("groups", "mp"), check_vma=False
    )
```

```python
import functools
import math

import jax
import jax.numpy as jnp
from jax import lax
from jax.experimental import pallas as pl
from jax.experimental.pallas import tpu as pltpu
from jax.sharding import PartitionSpec as P

HEAD = 64
CH = 64
TILE = 4
LANES = 128
PACK = 16

GUIDE = 3.5
STEP = -0.25
EPS = 1e-06
LOG2E = 1.4426950408889634
DEAD = -1e30
SEND_MIB, PREPARE_MIB, ATTEND_MIB, FINISH_MIB, UPDATE_MIB = 60, 56, 52, 24, 16

F32 = jnp.float32
BF16 = jnp.bfloat16
MIB = 2**20


def round_up(value, step):
    return (value + step - 1) // step * step


def spans(total, step):
    return [(start, min(start + step, total)) for start in range(0, total, step)]


def mm(left, right):
    return jnp.dot(left, right, preferred_element_type=F32)


def mm_nt(left, right):
    return lax.dot_general(left, right, (((1,), (1,)), ((), ())), preferred_element_type=F32)


def mm_tn(left, right):
    return lax.dot_general(left, right, (((0,), (0,)), ((), ())), preferred_element_type=F32)


def iota(shape, dim):
    return lax.broadcasted_iota(jnp.int32, shape, dim)


def two_terms(value):
    high = value.astype(BF16)
    return high, (value - high.astype(F32)).astype(BF16)


def one_hot(mask):
    return jnp.where(mask, 1.0, 0.0).astype(BF16)


def spec(space=pltpu.VMEM):
    return pl.BlockSpec(memory_space=space)


def grant(mib):
    return pltpu.CompilerParams(vmem_limit_bytes=mib * MIB)


def position():
    return lax.axis_index("groups").astype(jnp.int32), lax.axis_index("mp").astype(jnp.int32)


def head_norm(value, gains):
    wide = value.shape[1]
    same = iota((wide, wide), 0) // HEAD == iota((wide, wide), 1) // HEAD
    averaging = jnp.where(same, 1.0 / HEAD, 0.0).astype(BF16)
    square = mm((value * value).astype(BF16), averaging)
    return value * (lax.rsqrt(square + EPS) * gains)


def lanes_of(gains, wide):
    return jnp.concatenate([gains] * (wide // HEAD), axis=1)


def column_of(gains_ref, index):
    row = jnp.broadcast_to(gains_ref[index : index + 1, :], (LANES, HEAD))
    return row.T[:, 0:1]


def head_norm_down(value, gains):
    parts = []
    for at in range(0, value.shape[0], HEAD):
        head = value[at : at + HEAD]
        square = jnp.sum(head * head, axis=0, keepdims=True) * (1.0 / HEAD)
        parts.append(head * lax.rsqrt(square + EPS) * gains)
    return jnp.concatenate(parts, axis=0)


def own_bucket(slots_ref, group, tiles):
    first = group * tiles
    row = first // LANES
    after = jnp.minimum(row + 1, slots_ref.shape[0] - 1)
    window = jnp.concatenate([slots_ref[pl.ds(row, 1), :], slots_ref[pl.ds(after, 1), :]], axis=1)
    turn = 2 * LANES - (first - row * LANES)
    slots = pltpu.roll(window, turn, 1)[:, :tiles]
    target = slots // tiles
    across = target.astype(F32)
    diagonal = iota((tiles, tiles), 0) == iota((tiles, tiles), 1)
    down = jnp.sum(jnp.where(diagonal, across, 0.0), axis=1, keepdims=True)
    earlier = (down == across) & (iota((tiles, tiles), 0) < iota((tiles, tiles), 1))
    rank = jnp.sum(jnp.where(earlier, 1.0, 0.0), axis=0, keepdims=True).astype(jnp.int32)
    return target, rank


def send_kernel(capacity, block, slots_ref, latents_ref, out_ref):
    tiles = latents_ref.shape[0]
    groups_n = out_ref.shape[0]
    group, _ = position()
    target, rank = own_bucket(slots_ref, group, tiles)
    rows = groups_n * block
    bucket = iota((rows, tiles), 0)
    first = target * block + rank
    second = (target ^ 1) * block + capacity + rank
    sender = one_hot((bucket == first) | (bucket == second))
    sent = mm(sender, latents_ref[...].astype(BF16)).astype(BF16).reshape(groups_n, block, -1)
    out_ref[:, 0] = sent
    out_ref[:, 1] = sent


def slots_by_group(slots_ref, tiles):
    per = LANES // math.gcd(tiles, LANES)
    rows_per = per * tiles // LANES
    repeats = slots_ref.shape[0] // rows_per
    wide = jnp.concatenate(
        [slots_ref[pl.ds(row, repeats, stride=rows_per), :] for row in range(rows_per)], axis=1
    )
    parts = [wide[:, turn * tiles : (turn + 1) * tiles] for turn in range(per)]
    return jnp.concatenate(parts, axis=0), lambda row: per * (row % repeats) + row // repeats


def tables(slots, group_of, group, capacity, block, offset):
    groups_n, tiles = slots.shape
    target = slots // tiles
    placed = slots - target * tiles
    mine = target == group
    before = one_hot(iota((tiles, tiles), 0) < iota((tiles, tiles), 1))
    rank = jnp.where(mine, mm(one_hot(mine), before), float(capacity))
    columns = groups_n * block
    spread = one_hot(iota((groups_n, columns), 1) // block == group_of(iota((groups_n, columns), 0)))
    rank_of = mm_tn(rank.astype(BF16), spread)
    place_of = mm_tn(placed.astype(F32).astype(BF16), spread)
    level = (iota((tiles, columns), 1) % block - offset).astype(F32)
    hit = (rank_of == level) & (level >= 0.0) & (level < capacity)
    place = jnp.sum(jnp.where(hit, place_of + 1.0, 0.0), axis=0, keepdims=True) - 1.0
    return one_hot(iota((tiles, columns), 0).astype(F32) == place)


def prepare_kernel(
    capacity,
    block,
    back,
    step,
    slots_hbm,
    embed_hbm,
    own_mod_hbm,
    mate_mod_hbm,
    gains_hbm,
    states_hbm,
    w_text_hbm,
    w_qkv_hbm,
    home_out,
    rows_hbm,
    turned_hbm,
    slots_ref,
    embed_ref,
    own_mod_ref,
    mate_mod_ref,
    gains_ref,
    rows_out,
    turned_out,
    states,
    mingled,
    w_qkv,
    wide,
    split,
    sums,
    left,
    sems,
    out_sems,
    small_sems,
):
    depth = embed_ref.shape[1]
    width = w_qkv.shape[2]
    text = states.shape[0]
    tiles = home_out.shape[0]
    group, _ = position()
    own_rows = 2 * CH
    half = own_rows + PACK
    fold_rows = 2 * CH + PACK
    chunks = spans(depth, step)
    lane_tiles = width // LANES

    small = (
        (embed_hbm, embed_ref),
        (own_mod_hbm, own_mod_ref),
        (mate_mod_hbm, mate_mod_ref),
        (slots_hbm, slots_ref),
        (gains_hbm, gains_ref),
    )
    small = [
        pltpu.make_async_copy(source, target, small_sems.at[index])
        for index, (source, target) in enumerate(small)
    ]
    for copy in small:
        copy.start()
    sources = []

    def qkv_source(part):
        for low, high in spans(depth, 2 * step):
            rows = pl.ds(low, high - low)
            sources.append((w_qkv_hbm.at[part, rows], w_qkv.at[part, rows]))
        return len(sources)

    query_end = qkv_source(0)
    sources.append((states_hbm, states))
    w_mingled = w_text_hbm.reshape(2 * depth, width)
    for low, high in chunks:
        rows = pl.ds(2 * low, 2 * (high - low))
        sources.append((w_mingled.at[rows], mingled.at[rows]))
    text_end = len(sources)
    qkv_source(1)
    value_end = qkv_source(2)
    copies = [
        pltpu.make_async_copy(source, target, sems.at[index])
        for index, (source, target) in enumerate(sources)
    ]
    for copy in copies:
        copy.start()

    def wait(first, last):
        for index in range(first, last):
            copies[index].wait()

    for copy in small:
        copy.wait()

    embed = embed_ref[...].astype(F32)
    centred = embed - jnp.mean(embed, axis=1, keepdims=True)
    for side, mod_ref in ((0, own_mod_ref), (1, mate_mod_ref)):
        base = side * half
        for branch in range(2):
            scaled = centred * (1.0 + mod_ref[1, branch : branch + 1, :])
            left[pl.ds(base + branch * CH, CH), :] = scaled.astype(BF16)
        high, low = two_terms(mod_ref[0])
        shifts = jnp.concatenate([high.astype(F32), low.astype(F32)], axis=0)
        shifts = jnp.concatenate([shifts, jnp.zeros((PACK - 4, depth), F32)], axis=0)
        left[pl.ds(base + own_rows, PACK), :] = shifts.astype(BF16)
    def pieces(product, base, branch):
        first = base + own_rows + branch
        bias = two_terms(product[first : first + 1] + product[first + 2 : first + 3])
        fold = two_terms(product[base + branch * CH : base + (branch + 1) * CH])
        return [part.astype(F32) for part in fold + bias]

    def keep(product, base, side, lanes):
        for branch in range(2):
            zeros = jnp.zeros((PACK - 2, product.shape[1]), F32)
            stacked = jnp.concatenate(pieces(product, base, branch) + [zeros], axis=0)
            at = side * fold_rows
            rows_out[branch, at : at + fold_rows, lanes] = stacked.astype(BF16)

    def keep_turned(product, base, kind, lanes):
        for branch in range(2):
            high, low, bias_high, bias_low = pieces(product, base, branch)
            zeros = jnp.zeros((CH - 2, product.shape[1]), F32)
            stacked = jnp.concatenate([high, low, high, bias_high, bias_low, zeros], axis=0)
            turned_out[branch, kind, lanes, :] = stacked.T.astype(BF16)

    shared = width // (2 * LANES) * (2 * LANES)
    main, edge = slice(0, shared), slice(shared, width)
    def gram_and_tables():
        high, low = two_terms(centred)
        parts = (mm_nt(high, high) + (mm_nt(high, low) + mm_nt(low, high))) * (1.0 / depth)
        top, rest = two_terms(parts)
        bottom = (parts - top.astype(F32) - rest.astype(F32)).astype(BF16)
        gram = jnp.concatenate([top, rest, bottom, jnp.zeros((CH, CH), BF16)], axis=1)
        turned_out[0, 4, 2 * tiles : 2 * tiles + CH, :] = gram
        slots, group_of = slots_by_group(slots_ref, tiles)
        lanes_n = turned_out.shape[3]
        for side in range(2):
            place = tables(slots, group_of, group ^ side, capacity, block, side * capacity)
            for turn, (low, high) in enumerate(spans(place.shape[1], lanes_n)):
                turned_out[0, 4 + turn, side * tiles : (side + 1) * tiles, 0 : high - low] = place[:, low:high]
        home_out[...] = tables(slots, group_of, group, capacity, back, 0)

    out_copies = []

    def put(source, target):
        out_copies.append(pltpu.make_async_copy(source, target, out_sems.at[len(out_copies)]))
        out_copies[-1].start()

    def divide():
        for turn, (low, high) in enumerate(chunks):
            at = query_end + 1 + turn
            wait(at, at + 1)
            count = high - low
            for index in range(lane_tiles):
                lanes = slice(index * LANES, (index + 1) * LANES)
                wide[index, 0 : 2 * count, :] = mingled[2 * low : 2 * high, lanes].astype(F32)
            for part in range(2):
                for index in range(lane_tiles):
                    lanes = slice(part * width + index * LANES, part * width + (index + 1) * LANES)
                    split[low:high, lanes] = wide[index, pl.ds(part, count, stride=2), :].astype(BF16)

    gram_and_tables()
    wait(0, query_end + 1)
    query_product = mm(left[0:half, :], w_qkv[0])
    divide()
    keep_turned(query_product, 0, 0, slice(0, width))

    product = mm(states[...].reshape(2 * text, depth), split[...])
    for index in range(2 * lane_tiles):
        sums[index] = product[:, index * LANES : (index + 1) * LANES]
    wait(text_end, value_end)
    key_product = mm(left[...], w_qkv[1, :, main])
    gains = column_of(gains_ref, 2)
    padding = jnp.zeros((turned_out.shape[3] - text, LANES), F32)
    for branch in range(2):
        for index in range(lane_tiles):
            lanes = slice(index * LANES, (index + 1) * LANES)
            rows = pl.ds(branch, text, stride=2)
            keys = jnp.concatenate([sums[index, rows, :], padding], axis=0).T
            turned_out[branch, 3, lanes, :] = head_norm_down(keys, gains).astype(BF16)
            values = jnp.concatenate([sums[lane_tiles + index, rows, :], padding], axis=0)
            rows_out[branch, 2 * fold_rows :, lanes] = values.astype(BF16)
    keep_turned(key_product, 0, 1, main)
    keep_turned(key_product, half, 2, main)
    value_product = mm(left[...], w_qkv[2, :, main])
    put(turned_out.at[0, pl.ds(4, turned_out.shape[1] - 4)], turned_hbm.at[0, pl.ds(4, turned_out.shape[1] - 4)])
    if shared < width:
        edge_product = mm(left[...], jnp.concatenate([w_qkv[1, :, edge], w_qkv[2, :, edge]], axis=1))
    keep(value_product, 0, 0, main)
    keep(value_product, half, 1, main)
    if shared < width:
        keys, values = edge_product[:, : width - shared], edge_product[:, width - shared :]
        keep_turned(keys, 0, 1, edge)
        keep_turned(keys, half, 2, edge)
        keep(values, 0, 0, edge)
        keep(values, half, 1, edge)
    for branch in range(2):
        put(turned_out.at[branch, pl.ds(0, 4)], turned_hbm.at[branch, pl.ds(0, 4)])
        put(rows_out.at[branch], rows_hbm.at[branch])
    for copy in out_copies:
        copy.wait()


def attend_kernel(
    live_ref,
    partner_ref,
    arrived_ref,
    gains_ref,
    rows_hbm,
    turned_hbm,
    keep_ref,
    send_ref,
    tokens_ref,
    rows_ref,
    turned_ref,
    queries,
    keys,
    values,
    sems,
    *,
    text,
):
    def fetch(source, target, index):
        copy = pltpu.make_async_copy(source, target, sems.at[index])
        copy.start()
        return copy

    tables_n = turned_hbm.shape[1] - 4
    tables_at = (0, pl.ds(4, tables_n))
    tables_copy = fetch(turned_hbm.at[tables_at], turned_ref.at[tables_at], 0)
    copies = [
        (
            fetch(turned_hbm.at[branch, pl.ds(0, 4)], turned_ref.at[branch, pl.ds(0, 4)], 1 + 2 * branch),
            fetch(rows_hbm.at[branch], rows_ref.at[branch], 2 + 2 * branch),
        )
        for branch in range(2)
    ]
    group, member = position()
    groups_n, _, block, narrow = arrived_ref.shape
    rest = turned_ref.shape[3]
    half_rows = tokens_ref.shape[0]
    rows = 2 * half_rows
    tiles = rows // TILE
    width = keep_ref.shape[2]
    fold_rows = 2 * CH + PACK
    mate = partner_ref[group]
    own_len = live_ref[group]
    mate_len = jnp.where(mate != group, live_ref[mate], 0)

    own_parts, mate_parts = [], []
    tables_copy.wait()
    gram = turned_ref[0, 4, 2 * tiles : 2 * tiles + CH, :]
    for turn in range(2):
        source = member ^ turn
        block_rows = arrived_ref[:, pl.ds(source, 1)].reshape(groups_n * block, narrow)
        found = sum(
            mm(turned_ref[0, 4 + turn, 0 : 2 * tiles, 0 : high - low], block_rows[low:high])
            for turn, (low, high) in enumerate(spans(groups_n * block, rest))
        )
        for parts, base in ((own_parts, 0), (mate_parts, tiles)):
            pair = found[base : base + tiles]
            parts.append(jnp.concatenate([pair[:, :CH], pair[:, :CH]], axis=1))
            parts.append(jnp.concatenate([pair[:, CH:], pair[:, CH:]], axis=1))
    own_tokens = jnp.concatenate(own_parts, axis=0)
    mate_tokens = jnp.concatenate(mate_parts, axis=0)
    tokens_ref[...] = own_tokens[:half_rows].astype(BF16)
    lane = iota((1, LANES), 1)

    def normed(tokens):
        image = mm(tokens[:, :CH].astype(BF16), gram)
        image = (image[:, :LANES] + image[:, LANES:]) * tokens
        variance = jnp.sum(image, axis=1, keepdims=True)
        scaled = tokens * lax.rsqrt(jnp.maximum(variance, 0.0) + EPS)
        high = scaled.astype(BF16).astype(F32)
        ones = jnp.where(lane < CH + 2, 1.0, 0.0)
        return jnp.concatenate([high, jnp.where(lane < CH, scaled - high, ones)], axis=1)

    own_normed = normed(own_tokens)
    mate_normed = normed(mate_tokens)
    own_turned = own_normed.T.astype(BF16)
    mate_turned = mate_normed.T.astype(BF16)
    own_normed = own_normed.astype(BF16)
    mate_normed = mate_normed.astype(BF16)

    row = iota((1, rows), 1)
    turn_of = row // half_rows
    inside = row - turn_of * half_rows
    second = inside // tiles
    slot = (inside - second * tiles) * TILE + 2 * (turn_of ^ member) + second
    own_dead = jnp.where(slot < own_len, 0.0, DEAD)
    mate_dead = jnp.where(slot < mate_len, 0.0, DEAD)
    text_dead = jnp.where(iota((1, rest), 1) < text, 0.0, DEAD)
    dead = jnp.concatenate([own_dead, mate_dead, text_dead], axis=1)
    dead = jnp.where(iota((PACK, 1), 0) == 0, dead, 0.0).astype(BF16)
    one_row = jnp.where(iota((PACK, rows), 0) == 0, 1.0, 0.0)

    even = lane < HEAD
    query_gains = column_of(gains_ref, 0) * (LOG2E * HEAD**-0.5)
    key_gains = column_of(gains_ref, 1)
    filling = jnp.zeros((CH - PACK, width), BF16)
    lane_tiles = width // LANES

    def fold_of(branch, side):
        fold = rows_ref[branch, side * fold_rows : (side + 1) * fold_rows, :]
        return jnp.concatenate([fold[: 2 * CH], fold[:CH], fold[2 * CH :], filling], axis=0)

    def project(branch):
        for copy in copies[branch]:
            copy.wait()
        query = head_norm_down(mm(turned_ref[branch, 0], own_turned), query_gains)
        for head in range(width // HEAD):
            stacked = jnp.concatenate([query[head * HEAD : (head + 1) * HEAD], one_row], axis=0)
            queries[branch, head] = stacked.T.astype(BF16)
        for side, turned in ((0, own_turned), (1, mate_turned)):
            key = head_norm_down(mm(turned_ref[branch, 1 + side], turned), key_gains)
            keys[branch, :, side * rows : (side + 1) * rows] = key.astype(BF16)
        keys[branch, :, 2 * rows :] = turned_ref[branch, 3]
        values[branch, 0:rows, :] = mm(own_normed, fold_of(branch, 0)).astype(BF16)
        values[branch, rows : 2 * rows, :] = mm(mate_normed, fold_of(branch, 1)).astype(BF16)
        values[branch, 2 * rows :, :] = rows_ref[branch, 2 * fold_rows :, :]

    def score(branch, at, side):
        first = at + side * HEAD
        one_keys = jnp.concatenate([keys[branch, first : first + HEAD, :], dead], axis=0)
        return mm(queries[branch, first // HEAD], one_keys)

    outs = []

    def settle(branch, at, side, scores):
        inside_head = even if side == 0 else jnp.logical_not(even)
        one_values = values[branch, :, at : at + LANES]
        one_values = jnp.where(inside_head, one_values, jnp.ones_like(one_values))
        highest = jnp.max(scores, axis=1, keepdims=True)
        outs.append(mm(jnp.exp2(scores - highest).astype(BF16), one_values))
        if side == 1:
            first, second = outs
            outs.clear()
            total = jnp.where(even, second, first)
            total = jnp.concatenate([total[:, HEAD:], total[:, :HEAD]], axis=1)
            merged = (jnp.where(even, first, second) / total).astype(BF16)
            keep_ref[branch, :, at : at + LANES] = merged[:half_rows]
            send_ref[branch, :, at : at + LANES] = merged[half_rows:]

    waiting = None
    project(0)
    for branch in range(2):
        for pair in range(lane_tiles):
            for side in range(2):
                at = pair * LANES
                scores = score(branch, at, side)
                if waiting is not None:
                    settle(*waiting)
                waiting = (branch, at, side, scores)
            if branch == 0 and pair == 0:
                project(1)
    settle(*waiting)


def finish_kernel(
    step,
    live_ref,
    kept_ref,
    came_ref,
    w_own_ref,
    w_came_ref,
    tokens_ref,
    embed_ref,
    mod_ref,
    w_final_ref,
    home_ref,
    out_ref,
    state,
):
    group, member = position()
    half_rows = tokens_ref.shape[0]
    tiles = home_ref.shape[0]
    width, depth = w_own_ref.shape
    both = 2 * half_rows
    chunks = spans(depth, step)
    attended = jnp.concatenate(
        [kept_ref[...].reshape(both, width), came_ref[...].reshape(both, width)], axis=1
    )

    def rows_of(index, low, high):
        first = jnp.broadcast_to(mod_ref[index, 0:1, low:high], (half_rows, high - low))
        second = jnp.broadcast_to(mod_ref[index, 1:2, low:high], (half_rows, high - low))
        return jnp.concatenate([first, second], axis=0)

    def folded(value):
        return sum(value[:, at : at + LANES] for at in range(0, value.shape[1], LANES))

    pivot = None
    total = jnp.zeros((both, LANES), F32)
    squares = jnp.zeros((both, LANES), F32)
    for low, high in chunks:
        weights = jnp.concatenate([w_own_ref[:, low:high], w_came_ref[:, low:high]], axis=0)
        mixed = mm(attended, weights)
        hidden = mm(tokens_ref[:, :CH], embed_ref[:, low:high])
        hidden = jnp.concatenate([hidden, hidden], axis=0)
        value = hidden + rows_of(2, low, high) * mixed
        if pivot is None:
            pivot = jnp.sum(folded(value), axis=1, keepdims=True) * (1.0 / (high - low))
        value = value - pivot
        state[:, low:high] = value
        total += folded(value)
        squares += folded(value * value)
    mean = jnp.sum(total, axis=1, keepdims=True) * (1.0 / depth)
    spread = jnp.sum(squares, axis=1, keepdims=True) * (1.0 / depth) - mean * mean
    scale = lax.rsqrt(jnp.maximum(spread, 0.0) + EPS)
    offset = -mean * scale
    velocity = jnp.zeros((both, CH), F32)
    for low, high in chunks:
        normed = state[:, low:high] * scale + offset
        final = normed * (1.0 + rows_of(4, low, high)) + rows_of(3, low, high)
        velocity += mm_nt(final.astype(BF16), w_final_ref[:, low:high])
    guided = velocity[half_rows:] + GUIDE * (velocity[:half_rows] - velocity[half_rows:])
    row = iota((half_rows, 1), 0)
    second = row // tiles
    slot = (row - second * tiles) * TILE + 2 * member + second
    guided = jnp.where(slot < live_ref[group], guided, 0.0)
    columns = jnp.concatenate([guided[:tiles], guided[tiles:]], axis=1).astype(BF16)
    out_ref[...] = mm_tn(home_ref[...], columns).astype(BF16)


def update_kernel(back, slots_ref, latents_ref, returned_ref, out_ref):
    tiles = latents_ref.shape[0]
    group, _ = position()
    target, rank = own_bucket(slots_ref, group, tiles)
    sender = one_hot(iota((returned_ref.shape[0], tiles), 0) == target * back + rank)
    out_ref[...] = latents_ref[...] + STEP * mm_tn(sender, returned_ref[...])


def shards(
    latents,
    tile_slot,
    live,
    partner,
    text_states,
    modulation,
    w_embed,
    w_qkv,
    w_text_kv,
    w_out,
    w_final,
    norm_gains,
):
    groups_n = lax.axis_size("groups")
    tiles, narrow = latents.shape
    rows = tiles * TILE
    depth = w_embed.shape[1]
    width = w_out.shape[0]
    text = text_states.shape[2]
    capacity = max(2, (tiles + groups_n - 1) // groups_n)
    block = round_up(2 * capacity, PACK)
    back = round_up(capacity, PACK)
    slots = tile_slot.reshape(groups_n * tiles // LANES, LANES)
    both = ("groups", "mp")
    cores = [(0, 1), (1, 0)]

    adaptive = jnp.swapaxes(modulation[0], 0, 1)
    pairs = [(source, source ^ 1) for source in range(groups_n)]
    mate_mod = lax.ppermute(adaptive, "groups", pairs)

    outbound = pl.pallas_call(
        functools.partial(send_kernel, capacity, block),
        out_shape=jax.ShapeDtypeStruct((groups_n, 2, block, narrow), BF16),
        in_specs=[spec(), spec()],
        out_specs=spec(),
        compiler_params=grant(SEND_MIB),
    )(slots, latents)
    arrived = lax.all_to_all(
        outbound.reshape(groups_n * 2, block, narrow), both, split_axis=0, concat_axis=0, tiled=True
    ).reshape(groups_n, 2, block, narrow)

    step = 4 * LANES
    chunk_n = len(spans(depth, step))
    qkv_n = len(spans(depth, 2 * step))
    left_rows = 2 * (2 * CH + PACK)
    rest = round_up(2 * rows + text, 2 * LANES) - 2 * rows
    rows_shape = (2, 2 * (2 * CH + PACK) + rest, width)
    turned_shape = (2, 4 + len(spans(groups_n * block, rest)), width, rest)
    home, rows_kit, turned_kit = pl.pallas_call(
        functools.partial(prepare_kernel, capacity, block, back, step),
        out_shape=[
            jax.ShapeDtypeStruct((tiles, groups_n * back), BF16),
            jax.ShapeDtypeStruct(rows_shape, BF16),
            jax.ShapeDtypeStruct(turned_shape, BF16),
        ],
        in_specs=[spec(pltpu.HBM)] * 8,
        out_specs=[spec()] + [spec(pltpu.HBM)] * 2,
        scratch_shapes=[
            pltpu.VMEM(slots.shape, jnp.int32),
            pltpu.VMEM(w_embed.shape, BF16),
            pltpu.VMEM(adaptive.shape, F32),
            pltpu.VMEM(adaptive.shape, F32),
            pltpu.VMEM(norm_gains.shape, F32),
            pltpu.VMEM(rows_shape, BF16),
            pltpu.VMEM(turned_shape, BF16),
            pltpu.VMEM((text, 2, depth), BF16),
            pltpu.VMEM((2 * depth, width), BF16),
            pltpu.VMEM((3, depth, width), BF16),
            pltpu.VMEM((width // LANES, 2 * step, LANES), F32),
            pltpu.VMEM((depth, 2 * width), BF16),
            pltpu.VMEM((2 * width // LANES, 2 * text, LANES), F32),
            pltpu.VMEM((left_rows, depth), BF16),
            pltpu.SemaphoreType.DMA((1 + chunk_n + 3 * qkv_n,)),
            pltpu.SemaphoreType.DMA((7,)),
            pltpu.SemaphoreType.DMA((5,)),
        ],
        compiler_params=grant(PREPARE_MIB),
        cost_estimate=pl.CostEstimate(
            flops=2 * (left_rows * 3 + 4 * text) * depth * width,
            bytes_accessed=2 * depth * 5 * width,
            transcendentals=0,
        ),
    )(
        slots,
        w_embed,
        adaptive,
        mate_mod,
        norm_gains,
        jnp.swapaxes(text_states[0], 0, 1),
        w_text_kv,
        jnp.swapaxes(w_qkv, 0, 1),
    )

    arrived, rows_kit, w_out_sent = lax.optimization_barrier((arrived, rows_kit, w_out))
    came_w_out = lax.ppermute(w_out_sent, "mp", cores)
    half = jax.ShapeDtypeStruct((2, rows // 2, width), BF16)
    kept, sent, tokens = pl.pallas_call(
        functools.partial(attend_kernel, text=text),
        out_shape=[half, half, jax.ShapeDtypeStruct((rows // 2, 2 * CH), BF16)],
        in_specs=[spec(pltpu.SMEM)] * 2 + [spec()] * 2 + [spec(pltpu.HBM)] * 2,
        out_specs=[spec()] * 3,
        scratch_shapes=[
            pltpu.VMEM(rows_shape, BF16),
            pltpu.VMEM(turned_shape, BF16),
            pltpu.VMEM((2, width // HEAD, rows, HEAD + PACK), BF16),
            pltpu.VMEM((2, width, 2 * rows + rest), BF16),
            pltpu.VMEM((2, 2 * rows + rest, width), BF16),
            pltpu.SemaphoreType.DMA((5,)),
        ],
        compiler_params=grant(ATTEND_MIB),
        cost_estimate=pl.CostEstimate(
            flops=40 * 2 * 2 * rows * (2 * rows + rest) * width,
            bytes_accessed=8 * MIB,
            transcendentals=0,
        ),
    )(live, partner, arrived, norm_gains, rows_kit, turned_kit)
    came = lax.ppermute(sent, "mp", cores)

    homeward = pl.pallas_call(
        functools.partial(finish_kernel, step),
        out_shape=jax.ShapeDtypeStruct((groups_n * back, narrow), BF16),
        in_specs=[spec(pltpu.SMEM)] + [spec()] * 9,
        out_specs=spec(),
        scratch_shapes=[
            pltpu.VMEM((rows, depth), F32),
        ],
        compiler_params=grant(FINISH_MIB),
    )(live, kept, came, w_out, came_w_out, tokens, w_embed, adaptive, w_final.T, home)
    returned = lax.all_to_all(
        homeward.reshape(groups_n, back, narrow), "groups", split_axis=0, concat_axis=0, tiled=True
    ).reshape(groups_n * back, narrow)
    return pl.pallas_call(
        functools.partial(update_kernel, back),
        out_shape=jax.ShapeDtypeStruct((tiles, narrow), F32),
        in_specs=[spec()] * 3,
        out_specs=spec(),
        compiler_params=grant(UPDATE_MIB),
    )(slots, latents, returned)


def solution(mesh):
    placed = (
        P("groups", "mp"),
        P(),
        P(),
        P(),
        P("groups", None, None, None),
        P("groups", None, None, None),
        P(),
        P(None, None, "mp"),
        P(None, None, "mp"),
        P("mp", None),
        P(),
        P(),
    )
    return jax.shard_map(
        shards, mesh=mesh, in_specs=placed, out_specs=P("groups", "mp"), check_vma=False
    )
```

```python
import functools
import math

import jax
import jax.numpy as jnp
from jax import lax
from jax.experimental import pallas as pl
from jax.experimental.pallas import tpu as pltpu
from jax.sharding import PartitionSpec as P

HEAD = 64
CH = 64
TILE = 4
LANES = 128
PACK = 16

GUIDE = 3.5
STEP = -0.25
EPS = 1e-06
LOG2E = 1.4426950408889634
DEAD = -1e30
SEND_MIB, PREPARE_MIB, ATTEND_MIB, FINISH_MIB, UPDATE_MIB = 60, 56, 52, 24, 16

F32 = jnp.float32
BF16 = jnp.bfloat16
MIB = 2**20


def round_up(value, step):
    return (value + step - 1) // step * step


def spans(total, step):
    return [(start, min(start + step, total)) for start in range(0, total, step)]


def mm(left, right):
    return jnp.dot(left, right, preferred_element_type=F32)


def mm_nt(left, right):
    return lax.dot_general(left, right, (((1,), (1,)), ((), ())), preferred_element_type=F32)


def mm_tn(left, right):
    return lax.dot_general(left, right, (((0,), (0,)), ((), ())), preferred_element_type=F32)


def iota(shape, dim):
    return lax.broadcasted_iota(jnp.int32, shape, dim)


def two_terms(value):
    high = value.astype(BF16)
    return high, (value - high.astype(F32)).astype(BF16)


def one_hot(mask):
    return jnp.where(mask, 1.0, 0.0).astype(BF16)


def spec(space=pltpu.VMEM):
    return pl.BlockSpec(memory_space=space)


def grant(mib):
    return pltpu.CompilerParams(vmem_limit_bytes=mib * MIB)


def position():
    return lax.axis_index("groups").astype(jnp.int32), lax.axis_index("mp").astype(jnp.int32)


def head_norm(value, gains):
    wide = value.shape[1]
    same = iota((wide, wide), 0) // HEAD == iota((wide, wide), 1) // HEAD
    averaging = jnp.where(same, 1.0 / HEAD, 0.0).astype(BF16)
    square = mm((value * value).astype(BF16), averaging)
    return value * (lax.rsqrt(square + EPS) * gains)


def lanes_of(gains, wide):
    return jnp.concatenate([gains] * (wide // HEAD), axis=1)


def column_of(gains_ref, index):
    row = jnp.broadcast_to(gains_ref[index : index + 1, :], (LANES, HEAD))
    return row.T[:, 0:1]


def head_norm_down(value, gains):
    parts = []
    for at in range(0, value.shape[0], HEAD):
        head = value[at : at + HEAD]
        square = jnp.sum(head * head, axis=0, keepdims=True) * (1.0 / HEAD)
        parts.append(head * lax.rsqrt(square + EPS) * gains)
    return jnp.concatenate(parts, axis=0)


def own_bucket(slots_ref, group, tiles):
    first = group * tiles
    row = first // LANES
    after = jnp.minimum(row + 1, slots_ref.shape[0] - 1)
    window = jnp.concatenate([slots_ref[pl.ds(row, 1), :], slots_ref[pl.ds(after, 1), :]], axis=1)
    turn = 2 * LANES - (first - row * LANES)
    slots = pltpu.roll(window, turn, 1)[:, :tiles]
    target = slots // tiles
    across = target.astype(F32)
    diagonal = iota((tiles, tiles), 0) == iota((tiles, tiles), 1)
    down = jnp.sum(jnp.where(diagonal, across, 0.0), axis=1, keepdims=True)
    earlier = (down == across) & (iota((tiles, tiles), 0) < iota((tiles, tiles), 1))
    rank = jnp.sum(jnp.where(earlier, 1.0, 0.0), axis=0, keepdims=True).astype(jnp.int32)
    return target, rank


def send_kernel(capacity, block, slots_ref, latents_ref, out_ref):
    tiles = latents_ref.shape[0]
    groups_n = out_ref.shape[0]
    group, _ = position()
    target, rank = own_bucket(slots_ref, group, tiles)
    rows = groups_n * block
    bucket = iota((rows, tiles), 0)
    first = target * block + rank
    second = (target ^ 1) * block + capacity + rank
    sender = one_hot((bucket == first) | (bucket == second))
    sent = mm(sender, latents_ref[...].astype(BF16)).astype(BF16).reshape(groups_n, block, -1)
    out_ref[:, 0] = sent
    out_ref[:, 1] = sent


def slots_by_group(slots_ref, tiles):
    per = LANES // math.gcd(tiles, LANES)
    rows_per = per * tiles // LANES
    repeats = slots_ref.shape[0] // rows_per
    wide = jnp.concatenate(
        [slots_ref[pl.ds(row, repeats, stride=rows_per), :] for row in range(rows_per)], axis=1
    )
    parts = [wide[:, turn * tiles : (turn + 1) * tiles] for turn in range(per)]
    return jnp.concatenate(parts, axis=0), lambda row: per * (row % repeats) + row // repeats


def tables(slots, group_of, group, capacity, block, offset):
    groups_n, tiles = slots.shape
    target = slots // tiles
    placed = slots - target * tiles
    mine = target == group
    before = one_hot(iota((tiles, tiles), 0) < iota((tiles, tiles), 1))
    rank = jnp.where(mine, mm(one_hot(mine), before), float(capacity))
    columns = groups_n * block
    spread = one_hot(iota((groups_n, columns), 1) // block == group_of(iota((groups_n, columns), 0)))
    rank_of = mm_tn(rank.astype(BF16), spread)
    place_of = mm_tn(placed.astype(F32).astype(BF16), spread)
    level = (iota((tiles, columns), 1) % block - offset).astype(F32)
    hit = (rank_of == level) & (level >= 0.0) & (level < capacity)
    place = jnp.sum(jnp.where(hit, place_of + 1.0, 0.0), axis=0, keepdims=True) - 1.0
    return one_hot(iota((tiles, columns), 0).astype(F32) == place)


def prepare_kernel(
    capacity,
    block,
    back,
    step,
    slots_hbm,
    embed_hbm,
    own_mod_hbm,
    mate_mod_hbm,
    gains_hbm,
    states_hbm,
    w_text_hbm,
    w_qkv_hbm,
    home_out,
    rows_hbm,
    turned_hbm,
    slots_ref,
    embed_ref,
    own_mod_ref,
    mate_mod_ref,
    gains_ref,
    rows_out,
    turned_out,
    states,
    mingled,
    w_qkv,
    wide,
    split,
    sums,
    left,
    sems,
    out_sems,
    small_sems,
):
    depth = embed_ref.shape[1]
    width = w_qkv.shape[2]
    text = states.shape[0]
    tiles = home_out.shape[0]
    group, _ = position()
    own_rows = 2 * CH
    half = own_rows + PACK
    fold_rows = 2 * CH + PACK
    chunks = spans(depth, step)
    lane_tiles = width // LANES

    small = (
        (embed_hbm, embed_ref),
        (own_mod_hbm, own_mod_ref),
        (mate_mod_hbm, mate_mod_ref),
        (slots_hbm, slots_ref),
        (gains_hbm, gains_ref),
    )
    small = [
        pltpu.make_async_copy(source, target, small_sems.at[index])
        for index, (source, target) in enumerate(small)
    ]
    for copy in small:
        copy.start()
    sources = []

    def qkv_source(part):
        for low, high in spans(depth, 2 * step):
            rows = pl.ds(low, high - low)
            sources.append((w_qkv_hbm.at[part, rows], w_qkv.at[part, rows]))
        return len(sources)

    query_end = qkv_source(0)
    sources.append((states_hbm, states))
    w_mingled = w_text_hbm.reshape(2 * depth, width)
    for low, high in chunks:
        rows = pl.ds(2 * low, 2 * (high - low))
        sources.append((w_mingled.at[rows], mingled.at[rows]))
    text_end = len(sources)
    qkv_source(1)
    value_end = qkv_source(2)
    copies = [
        pltpu.make_async_copy(source, target, sems.at[index])
        for index, (source, target) in enumerate(sources)
    ]
    for copy in copies:
        copy.start()

    def wait(first, last):
        for index in range(first, last):
            copies[index].wait()

    for copy in small:
        copy.wait()

    embed = embed_ref[...].astype(F32)
    centred = embed - jnp.mean(embed, axis=1, keepdims=True)
    for side, mod_ref in ((0, own_mod_ref), (1, mate_mod_ref)):
        base = side * half
        for branch in range(2):
            scaled = centred * (1.0 + mod_ref[1, branch : branch + 1, :])
            left[pl.ds(base + branch * CH, CH), :] = scaled.astype(BF16)
        high, low = two_terms(mod_ref[0])
        shifts = jnp.concatenate([high.astype(F32), low.astype(F32)], axis=0)
        shifts = jnp.concatenate([shifts, jnp.zeros((PACK - 4, depth), F32)], axis=0)
        left[pl.ds(base + own_rows, PACK), :] = shifts.astype(BF16)
    def pieces(product, base, branch):
        first = base + own_rows + branch
        bias = two_terms(product[first : first + 1] + product[first + 2 : first + 3])
        fold = two_terms(product[base + branch * CH : base + (branch + 1) * CH])
        return [part.astype(F32) for part in fold + bias]

    def keep(product, base, side, lanes):
        for branch in range(2):
            zeros = jnp.zeros((PACK - 2, product.shape[1]), F32)
            stacked = jnp.concatenate(pieces(product, base, branch) + [zeros], axis=0)
            at = side * fold_rows
            rows_out[branch, at : at + fold_rows, lanes] = stacked.astype(BF16)

    def keep_turned(product, base, kind, lanes):
        for branch in range(2):
            high, low, bias_high, bias_low = pieces(product, base, branch)
            zeros = jnp.zeros((CH - 2, product.shape[1]), F32)
            stacked = jnp.concatenate([high, low, high, bias_high, bias_low, zeros], axis=0)
            turned_out[branch, kind, lanes, :] = stacked.T.astype(BF16)

    shared = width // (2 * LANES) * (2 * LANES)
    main, edge = slice(0, shared), slice(shared, width)
    def gram_and_tables():
        high, low = two_terms(centred)
        parts = (mm_nt(high, high) + (mm_nt(high, low) + mm_nt(low, high))) * (1.0 / depth)
        top, rest = two_terms(parts)
        bottom = (parts - top.astype(F32) - rest.astype(F32)).astype(BF16)
        gram = jnp.concatenate([top, rest, bottom, jnp.zeros((CH, CH), BF16)], axis=1)
        turned_out[0, 4, 2 * tiles : 2 * tiles + CH, :] = gram
        slots, group_of = slots_by_group(slots_ref, tiles)
        lanes_n = turned_out.shape[3]
        for side in range(2):
            place = tables(slots, group_of, group ^ side, capacity, block, side * capacity)
            for turn, (low, high) in enumerate(spans(place.shape[1], lanes_n)):
                turned_out[0, 4 + turn, side * tiles : (side + 1) * tiles, 0 : high - low] = place[:, low:high]
        home_out[...] = tables(slots, group_of, group, capacity, back, 0)

    out_copies = []

    def put(source, target):
        out_copies.append(pltpu.make_async_copy(source, target, out_sems.at[len(out_copies)]))
        out_copies[-1].start()

    def divide():
        for turn, (low, high) in enumerate(chunks):
            at = query_end + 1 + turn
            wait(at, at + 1)
            count = high - low
            for index in range(lane_tiles):
                lanes = slice(index * LANES, (index + 1) * LANES)
                wide[index, 0 : 2 * count, :] = mingled[2 * low : 2 * high, lanes].astype(F32)
            for part in range(2):
                for index in range(lane_tiles):
                    lanes = slice(part * width + index * LANES, part * width + (index + 1) * LANES)
                    split[low:high, lanes] = wide[index, pl.ds(part, count, stride=2), :].astype(BF16)

    gram_and_tables()
    wait(0, query_end + 1)
    query_product = mm(left[0:half, :], w_qkv[0])
    divide()
    keep_turned(query_product, 0, 0, slice(0, width))

    product = mm(states[...].reshape(2 * text, depth), split[...])
    for index in range(2 * lane_tiles):
        sums[index] = product[:, index * LANES : (index + 1) * LANES]
    wait(text_end, value_end)
    key_product = mm(left[...], w_qkv[1, :, main])
    gains = column_of(gains_ref, 2)
    padding = jnp.zeros((turned_out.shape[3] - text, LANES), F32)
    for branch in range(2):
        for index in range(lane_tiles):
            lanes = slice(index * LANES, (index + 1) * LANES)
            rows = pl.ds(branch, text, stride=2)
            keys = jnp.concatenate([sums[index, rows, :], padding], axis=0).T
            turned_out[branch, 3, lanes, :] = head_norm_down(keys, gains).astype(BF16)
            values = jnp.concatenate([sums[lane_tiles + index, rows, :], padding], axis=0)
            rows_out[branch, 2 * fold_rows :, lanes] = values.astype(BF16)
    keep_turned(key_product, 0, 1, main)
    keep_turned(key_product, half, 2, main)
    value_product = mm(left[...], w_qkv[2, :, main])
    put(turned_out.at[0, pl.ds(4, turned_out.shape[1] - 4)], turned_hbm.at[0, pl.ds(4, turned_out.shape[1] - 4)])
    if shared < width:
        edge_product = mm(left[...], jnp.concatenate([w_qkv[1, :, edge], w_qkv[2, :, edge]], axis=1))
    keep(value_product, 0, 0, main)
    keep(value_product, half, 1, main)
    if shared < width:
        keys, values = edge_product[:, : width - shared], edge_product[:, width - shared :]
        keep_turned(keys, 0, 1, edge)
        keep_turned(keys, half, 2, edge)
        keep(values, 0, 0, edge)
        keep(values, half, 1, edge)
    for branch in range(2):
        put(turned_out.at[branch, pl.ds(0, 4)], turned_hbm.at[branch, pl.ds(0, 4)])
        put(rows_out.at[branch], rows_hbm.at[branch])
    for copy in out_copies:
        copy.wait()


def attend_kernel(
    live_ref,
    partner_ref,
    arrived_ref,
    gains_ref,
    rows_hbm,
    turned_hbm,
    keep_ref,
    send_ref,
    tokens_ref,
    rows_ref,
    turned_ref,
    queries,
    keys,
    values,
    sems,
    *,
    text,
):
    def fetch(source, target, index):
        copy = pltpu.make_async_copy(source, target, sems.at[index])
        copy.start()
        return copy

    tables_n = turned_hbm.shape[1] - 4
    tables_at = (0, pl.ds(4, tables_n))
    tables_copy = fetch(turned_hbm.at[tables_at], turned_ref.at[tables_at], 0)
    copies = [
        (
            fetch(turned_hbm.at[branch, pl.ds(0, 4)], turned_ref.at[branch, pl.ds(0, 4)], 1 + 2 * branch),
            fetch(rows_hbm.at[branch], rows_ref.at[branch], 2 + 2 * branch),
        )
        for branch in range(2)
    ]
    group, member = position()
    groups_n, _, block, narrow = arrived_ref.shape
    rest = turned_ref.shape[3]
    half_rows = tokens_ref.shape[0]
    rows = 2 * half_rows
    tiles = rows // TILE
    width = keep_ref.shape[2]
    fold_rows = 2 * CH + PACK
    mate = partner_ref[group]
    own_len = live_ref[group]
    mate_len = jnp.where(mate != group, live_ref[mate], 0)

    own_parts, mate_parts = [], []
    tables_copy.wait()
    gram = turned_ref[0, 4, 2 * tiles : 2 * tiles + CH, :]
    for turn in range(2):
        source = member ^ turn
        block_rows = arrived_ref[:, pl.ds(source, 1)].reshape(groups_n * block, narrow)
        found = sum(
            mm(turned_ref[0, 4 + turn, 0 : 2 * tiles, 0 : high - low], block_rows[low:high])
            for turn, (low, high) in enumerate(spans(groups_n * block, rest))
        )
        for parts, base in ((own_parts, 0), (mate_parts, tiles)):
            pair = found[base : base + tiles]
            parts.append(jnp.concatenate([pair[:, :CH], pair[:, :CH]], axis=1))
            parts.append(jnp.concatenate([pair[:, CH:], pair[:, CH:]], axis=1))
    own_tokens = jnp.concatenate(own_parts, axis=0)
    mate_tokens = jnp.concatenate(mate_parts, axis=0)
    tokens_ref[...] = own_tokens[:half_rows].astype(BF16)
    lane = iota((1, LANES), 1)

    def normed(tokens):
        image = mm(tokens[:, :CH].astype(BF16), gram)
        image = (image[:, :LANES] + image[:, LANES:]) * tokens
        variance = jnp.sum(image, axis=1, keepdims=True)
        scaled = tokens * lax.rsqrt(jnp.maximum(variance, 0.0) + EPS)
        high = scaled.astype(BF16).astype(F32)
        ones = jnp.where(lane < CH + 2, 1.0, 0.0)
        return jnp.concatenate([high, jnp.where(lane < CH, scaled - high, ones)], axis=1)

    own_normed = normed(own_tokens)
    mate_normed = normed(mate_tokens)
    own_turned = own_normed.T.astype(BF16)
    mate_turned = mate_normed.T.astype(BF16)
    own_normed = own_normed.astype(BF16)
    mate_normed = mate_normed.astype(BF16)

    row = iota((1, rows), 1)
    turn_of = row // half_rows
    inside = row - turn_of * half_rows
    second = inside // tiles
    slot = (inside - second * tiles) * TILE + 2 * (turn_of ^ member) + second
    own_dead = jnp.where(slot < own_len, 0.0, DEAD)
    mate_dead = jnp.where(slot < mate_len, 0.0, DEAD)
    text_dead = jnp.where(iota((1, rest), 1) < text, 0.0, DEAD)
    dead = jnp.concatenate([own_dead, mate_dead, text_dead], axis=1)
    dead = jnp.where(iota((PACK, 1), 0) == 0, dead, 0.0).astype(BF16)
    one_row = jnp.where(iota((PACK, rows), 0) == 0, 1.0, 0.0)

    even = lane < HEAD
    query_gains = column_of(gains_ref, 0) * (LOG2E * HEAD**-0.5)
    key_gains = column_of(gains_ref, 1)
    filling = jnp.zeros((CH - PACK, width), BF16)
    lane_tiles = width // LANES

    def fold_of(branch, side):
        fold = rows_ref[branch, side * fold_rows : (side + 1) * fold_rows, :]
        return jnp.concatenate([fold[: 2 * CH], fold[:CH], fold[2 * CH :], filling], axis=0)

    def project(branch):
        for copy in copies[branch]:
            copy.wait()
        query = head_norm_down(mm(turned_ref[branch, 0], own_turned), query_gains)
        for head in range(width // HEAD):
            stacked = jnp.concatenate([query[head * HEAD : (head + 1) * HEAD], one_row], axis=0)
            queries[branch, head] = stacked.T.astype(BF16)
        for side, turned in ((0, own_turned), (1, mate_turned)):
            key = head_norm_down(mm(turned_ref[branch, 1 + side], turned), key_gains)
            keys[branch, :, side * rows : (side + 1) * rows] = key.astype(BF16)
        keys[branch, :, 2 * rows :] = turned_ref[branch, 3]
        values[branch, 0:rows, :] = mm(own_normed, fold_of(branch, 0)).astype(BF16)
        values[branch, rows : 2 * rows, :] = mm(mate_normed, fold_of(branch, 1)).astype(BF16)
        values[branch, 2 * rows :, :] = rows_ref[branch, 2 * fold_rows :, :]

    def score(branch, at, side):
        first = at + side * HEAD
        one_keys = jnp.concatenate([keys[branch, first : first + HEAD, :], dead], axis=0)
        return mm(queries[branch, first // HEAD], one_keys)

    outs = []

    def settle(branch, at, side, scores):
        inside_head = even if side == 0 else jnp.logical_not(even)
        one_values = values[branch, :, at : at + LANES]
        one_values = jnp.where(inside_head, one_values, jnp.ones_like(one_values))
        highest = jnp.max(scores, axis=1, keepdims=True)
        outs.append(mm(jnp.exp2(scores - highest).astype(BF16), one_values))
        if side == 1:
            first, second = outs
            outs.clear()
            total = jnp.where(even, second, first)
            total = jnp.concatenate([total[:, HEAD:], total[:, :HEAD]], axis=1)
            merged = (jnp.where(even, first, second) / total).astype(BF16)
            keep_ref[branch, :, at : at + LANES] = merged[:half_rows]
            send_ref[branch, :, at : at + LANES] = merged[half_rows:]

    waiting = None
    project(0)
    for branch in range(2):
        for pair in range(lane_tiles):
            for side in range(2):
                at = pair * LANES
                scores = score(branch, at, side)
                if waiting is not None:
                    settle(*waiting)
                waiting = (branch, at, side, scores)
            if branch == 0 and pair == 0:
                project(1)
    settle(*waiting)


def begin_kernel(step, kept_ref, w_own_ref, out_ref):
    width, depth = w_own_ref.shape
    kept = kept_ref[...].reshape(out_ref.shape[0], width)
    for low, high in spans(depth, step):
        out_ref[:, low:high] = mm(kept, w_own_ref[:, low:high])


def finish_kernel(
    step,
    live_ref,
    begun_ref,
    came_ref,
    w_came_ref,
    tokens_ref,
    embed_ref,
    mod_ref,
    w_final_ref,
    home_ref,
    out_ref,
    state,
):
    group, member = position()
    half_rows = tokens_ref.shape[0]
    tiles = home_ref.shape[0]
    width, depth = w_came_ref.shape
    both = 2 * half_rows
    chunks = spans(depth, step)
    came = came_ref[...].reshape(both, width)

    def rows_of(index, low, high):
        first = jnp.broadcast_to(mod_ref[index, 0:1, low:high], (half_rows, high - low))
        second = jnp.broadcast_to(mod_ref[index, 1:2, low:high], (half_rows, high - low))
        return jnp.concatenate([first, second], axis=0)

    def folded(value):
        return sum(value[:, at : at + LANES] for at in range(0, value.shape[1], LANES))

    pivot = None
    total = jnp.zeros((both, LANES), F32)
    squares = jnp.zeros((both, LANES), F32)
    for low, high in chunks:
        mixed = begun_ref[:, low:high] + mm(came, w_came_ref[:, low:high])
        hidden = mm(tokens_ref[:, :CH], embed_ref[:, low:high])
        hidden = jnp.concatenate([hidden, hidden], axis=0)
        value = hidden + rows_of(2, low, high) * mixed
        if pivot is None:
            pivot = jnp.sum(folded(value), axis=1, keepdims=True) * (1.0 / (high - low))
        value = value - pivot
        state[:, low:high] = value
        total += folded(value)
        squares += folded(value * value)
    mean = jnp.sum(total, axis=1, keepdims=True) * (1.0 / depth)
    spread = jnp.sum(squares, axis=1, keepdims=True) * (1.0 / depth) - mean * mean
    scale = lax.rsqrt(jnp.maximum(spread, 0.0) + EPS)
    offset = -mean * scale
    velocity = jnp.zeros((both, CH), F32)
    for low, high in chunks:
        normed = state[:, low:high] * scale + offset
        final = normed * (1.0 + rows_of(4, low, high)) + rows_of(3, low, high)
        velocity += mm_nt(final.astype(BF16), w_final_ref[:, low:high])
    guided = velocity[half_rows:] + GUIDE * (velocity[:half_rows] - velocity[half_rows:])
    row = iota((half_rows, 1), 0)
    second = row // tiles
    slot = (row - second * tiles) * TILE + 2 * member + second
    guided = jnp.where(slot < live_ref[group], guided, 0.0)
    columns = jnp.concatenate([guided[:tiles], guided[tiles:]], axis=1).astype(BF16)
    out_ref[...] = mm_tn(home_ref[...], columns).astype(BF16)


def update_kernel(back, slots_ref, latents_ref, returned_ref, out_ref):
    tiles = latents_ref.shape[0]
    group, _ = position()
    target, rank = own_bucket(slots_ref, group, tiles)
    sender = one_hot(iota((returned_ref.shape[0], tiles), 0) == target * back + rank)
    out_ref[...] = latents_ref[...] + STEP * mm_tn(sender, returned_ref[...])


def shards(
    latents,
    tile_slot,
    live,
    partner,
    text_states,
    modulation,
    w_embed,
    w_qkv,
    w_text_kv,
    w_out,
    w_final,
    norm_gains,
):
    groups_n = lax.axis_size("groups")
    tiles, narrow = latents.shape
    rows = tiles * TILE
    depth = w_embed.shape[1]
    width = w_out.shape[0]
    text = text_states.shape[2]
    capacity = max(2, (tiles + groups_n - 1) // groups_n)
    block = round_up(2 * capacity, PACK)
    back = round_up(capacity, PACK)
    slots = tile_slot.reshape(groups_n * tiles // LANES, LANES)
    both = ("groups", "mp")
    cores = [(0, 1), (1, 0)]

    adaptive = jnp.swapaxes(modulation[0], 0, 1)
    pairs = [(source, source ^ 1) for source in range(groups_n)]
    mate_mod = lax.ppermute(adaptive, "groups", pairs)

    outbound = pl.pallas_call(
        functools.partial(send_kernel, capacity, block),
        out_shape=jax.ShapeDtypeStruct((groups_n, 2, block, narrow), BF16),
        in_specs=[spec(), spec()],
        out_specs=spec(),
        compiler_params=grant(SEND_MIB),
    )(slots, latents)
    arrived = lax.all_to_all(
        outbound.reshape(groups_n * 2, block, narrow), both, split_axis=0, concat_axis=0, tiled=True
    ).reshape(groups_n, 2, block, narrow)

    step = 4 * LANES
    chunk_n = len(spans(depth, step))
    qkv_n = len(spans(depth, 2 * step))
    left_rows = 2 * (2 * CH + PACK)
    rest = round_up(2 * rows + text, 2 * LANES) - 2 * rows
    rows_shape = (2, 2 * (2 * CH + PACK) + rest, width)
    turned_shape = (2, 4 + len(spans(groups_n * block, rest)), width, rest)
    home, rows_kit, turned_kit = pl.pallas_call(
        functools.partial(prepare_kernel, capacity, block, back, step),
        out_shape=[
            jax.ShapeDtypeStruct((tiles, groups_n * back), BF16),
            jax.ShapeDtypeStruct(rows_shape, BF16),
            jax.ShapeDtypeStruct(turned_shape, BF16),
        ],
        in_specs=[spec(pltpu.HBM)] * 8,
        out_specs=[spec()] + [spec(pltpu.HBM)] * 2,
        scratch_shapes=[
            pltpu.VMEM(slots.shape, jnp.int32),
            pltpu.VMEM(w_embed.shape, BF16),
            pltpu.VMEM(adaptive.shape, F32),
            pltpu.VMEM(adaptive.shape, F32),
            pltpu.VMEM(norm_gains.shape, F32),
            pltpu.VMEM(rows_shape, BF16),
            pltpu.VMEM(turned_shape, BF16),
            pltpu.VMEM((text, 2, depth), BF16),
            pltpu.VMEM((2 * depth, width), BF16),
            pltpu.VMEM((3, depth, width), BF16),
            pltpu.VMEM((width // LANES, 2 * step, LANES), F32),
            pltpu.VMEM((depth, 2 * width), BF16),
            pltpu.VMEM((2 * width // LANES, 2 * text, LANES), F32),
            pltpu.VMEM((left_rows, depth), BF16),
            pltpu.SemaphoreType.DMA((1 + chunk_n + 3 * qkv_n,)),
            pltpu.SemaphoreType.DMA((7,)),
            pltpu.SemaphoreType.DMA((5,)),
        ],
        compiler_params=grant(PREPARE_MIB),
        cost_estimate=pl.CostEstimate(
            flops=2 * (left_rows * 3 + 4 * text) * depth * width,
            bytes_accessed=2 * depth * 5 * width,
            transcendentals=0,
        ),
    )(
        slots,
        w_embed,
        adaptive,
        mate_mod,
        norm_gains,
        jnp.swapaxes(text_states[0], 0, 1),
        w_text_kv,
        jnp.swapaxes(w_qkv, 0, 1),
    )

    arrived, rows_kit, w_out_sent = lax.optimization_barrier((arrived, rows_kit, w_out))
    came_w_out = lax.ppermute(w_out_sent, "mp", cores)
    half = jax.ShapeDtypeStruct((2, rows // 2, width), BF16)
    kept, sent, tokens = pl.pallas_call(
        functools.partial(attend_kernel, text=text),
        out_shape=[half, half, jax.ShapeDtypeStruct((rows // 2, 2 * CH), BF16)],
        in_specs=[spec(pltpu.SMEM)] * 2 + [spec()] * 2 + [spec(pltpu.HBM)] * 2,
        out_specs=[spec()] * 3,
        scratch_shapes=[
            pltpu.VMEM(rows_shape, BF16),
            pltpu.VMEM(turned_shape, BF16),
            pltpu.VMEM((2, width // HEAD, rows, HEAD + PACK), BF16),
            pltpu.VMEM((2, width, 2 * rows + rest), BF16),
            pltpu.VMEM((2, 2 * rows + rest, width), BF16),
            pltpu.SemaphoreType.DMA((5,)),
        ],
        compiler_params=grant(ATTEND_MIB),
        cost_estimate=pl.CostEstimate(
            flops=40 * 2 * 2 * rows * (2 * rows + rest) * width,
            bytes_accessed=8 * MIB,
            transcendentals=0,
        ),
    )(live, partner, arrived, norm_gains, rows_kit, turned_kit)
    came = lax.ppermute(sent, "mp", cores)

    begun = pl.pallas_call(
        functools.partial(begin_kernel, step),
        out_shape=jax.ShapeDtypeStruct((rows, depth), F32),
        in_specs=[spec()] * 2,
        out_specs=spec(),
        compiler_params=grant(FINISH_MIB),
        cost_estimate=pl.CostEstimate(
            flops=2 * rows * depth * width, bytes_accessed=8 * MIB, transcendentals=0
        ),
    )(kept, w_out)
    homeward = pl.pallas_call(
        functools.partial(finish_kernel, step),
        out_shape=jax.ShapeDtypeStruct((groups_n * back, narrow), BF16),
        in_specs=[spec(pltpu.SMEM)] + [spec()] * 8,
        out_specs=spec(),
        scratch_shapes=[
            pltpu.VMEM((rows, depth), F32),
        ],
        compiler_params=grant(FINISH_MIB),
    )(live, begun, came, came_w_out, tokens, w_embed, adaptive, w_final.T, home)
    returned = lax.all_to_all(
        homeward.reshape(groups_n, back, narrow), "groups", split_axis=0, concat_axis=0, tiled=True
    ).reshape(groups_n * back, narrow)
    return pl.pallas_call(
        functools.partial(update_kernel, back),
        out_shape=jax.ShapeDtypeStruct((tiles, narrow), F32),
        in_specs=[spec()] * 3,
        out_specs=spec(),
        compiler_params=grant(UPDATE_MIB),
    )(slots, latents, returned)


def solution(mesh):
    placed = (
        P("groups", "mp"),
        P(),
        P(),
        P(),
        P("groups", None, None, None),
        P("groups", None, None, None),
        P(),
        P(None, None, "mp"),
        P(None, None, "mp"),
        P("mp", None),
        P(),
        P(),
    )
    return jax.shard_map(
        shards, mesh=mesh, in_specs=placed, out_specs=P("groups", "mp"), check_vma=False
    )
```
